128 devices in a mesh: row: 16 (over z, x), col: 8 (over y, core).
Axes of the slice: x: 4, y: 4, z: 4, core: 2. Of those that a mesh axis runs over, the one named last changes fastest.
Arguments:
- blocks: float32 [8192, 4, 128, 128], P(('row', 'col')), may hold values from -0.25 to 0.25
- block_cols: int32 [8192, 4], P(('row', 'col')), may hold values from 0 to 1023, as said below
- targets: float32 [32, 1048576], P(None, ('row', 'col')), may hold values from -6 to 6
Outputs:
- solution: float32 [32, 131072], P(None, ('row', 'col'))
- residual: float32 [32, 1048576], P(None, ('row', 'col'))
The draws below stay inside these ranges and needn't reach their ends.
Inputs may be any that keep to these rules, and one draw needn't show every extreme that they name: `block_cols`: the four indices of a block row differ. Block row i belongs to device d = i // 64, devices numbered row-major over (row, col); every index j of it satisfies (j // 8) % 8 == d % 8.
All inputs are finite; a program needn't handle non-finite values.
Results may differ from the reference program's by a relative error of at most 0.00012.
Values sent between devices are 32-bit elements; how exact they have to be, the bound alone decides.
A program may use at most 128 MiB of HBM per device.

```python
import jax
import jax.numpy as jnp
from jax import lax

BS = 128
NRHS = 32
ITERS = 3
BRD = 64
CBD = 8
NBR = 8192
NBC = 1024
ROWS = 1048576
PARAMS = 131072
N_ROW = 16
N_COL = 8


def draw_block_cols(key, part):
    key = jax.random.fold_in(key, 5)
    first_key, second_key = jax.random.split(key)
    row_ids = jnp.arange(NBR, dtype=jnp.int32)
    col_group = row_ids // BRD % N_COL
    group_size = CBD * N_ROW
    quarter = group_size // 4
    base = jax.random.randint(first_key, (NBR, 1), 0, group_size, dtype=jnp.int32)
    offsets = jax.random.randint(second_key, (NBR, 4), 0, quarter, dtype=jnp.int32)
    local_ids = (base + jnp.arange(4, dtype=jnp.int32)[None, :] * quarter + offsets) % group_size
    result = (local_ids // CBD * N_COL + col_group[:, None]) * CBD + local_ids % CBD
    return result.astype(jnp.int32)


def level_of(rng, shape, cuts, smallest, largest):
    factor_of = 1.0
    for axis_at, blocks in cuts:
        heights = jax.random.uniform(jax.random.fold_in(jax.random.fold_in(rng, 6), axis_at), (blocks,), jnp.float32, smallest / len(cuts), largest / len(cuts))
        factor_of = factor_of * jnp.repeat(jnp.exp(heights), shape[axis_at] // blocks).reshape((-1,) + (1,) * (len(shape) - 1 - axis_at))
    return factor_of


def bell_draw(own_key, shape, deviation, reach, cuts=(), kind=jnp.bfloat16):
    level = level_of(own_key, shape, cuts, -0.22, 0.18) if cuts else 1.0
    values = jax.random.normal(own_key, shape, jnp.float32) * deviation * level
    return jnp.minimum(jnp.maximum(values, -reach), reach).astype(kind)


def setup_inputs(seed: int = 0) -> dict:
    arg_keys = jax.random.split(jax.random.key(seed), 4)
    return {
        "blocks": bell_draw(arg_keys[0], (NBR, 4, BS, BS), (4 * BS) ** -0.5, 0.25, ((0, 128),), jnp.float32),
        "block_cols": draw_block_cols(jax.random.fold_in(arg_keys[3], 71), 0),
        "targets": bell_draw(arg_keys[2], (NRHS, ROWS), 1.0, 6.0, ((1, 128),), jnp.float32),
    }


def chol_solve(matrix, right):
    lower_factor = jnp.linalg.cholesky(matrix)
    middle = lax.linalg.triangular_solve(lower_factor, right, left_side=True, lower=True)
    return lax.linalg.triangular_solve(lower_factor, middle, left_side=True, lower=True, transpose_a=True)

def apply_forward(blocks, block_cols, direction):
    rhs_count = direction.shape[0]
    tiles = direction.reshape(rhs_count, -1, BS)
    picked = jnp.take(tiles, block_cols.reshape(-1), axis=1)
    picked = picked.reshape(rhs_count, block_cols.shape[0], 4, BS)
    image = jnp.einsum('ikab,nikb->nia', blocks, picked, precision=lax.Precision.HIGHEST)
    return image.reshape(rhs_count, -1)

def apply_backward(blocks, block_cols, residual, segments):
    rhs_count = residual.shape[0]
    shaped = residual.reshape(rhs_count, blocks.shape[0], BS)
    pieces_all = jnp.einsum('ikab,nia->iknb', blocks, shaped, precision=lax.Precision.HIGHEST)
    pieces_all = pieces_all.reshape(-1, rhs_count, BS)
    summed = jax.ops.segment_sum(pieces_all, block_cols.reshape(-1), num_segments=segments)
    return summed.transpose(1, 0, 2).reshape(rhs_count, -1)

def gram_of(matrix):
    return jnp.dot(matrix.astype(jnp.float32), matrix.T.astype(jnp.float32), precision=lax.Precision.HIGHEST, preferred_element_type=jnp.float32)

def reference(blocks, block_cols, targets):
    residual = targets
    solution = jnp.zeros((NRHS, PARAMS), jnp.float32)
    gradient = apply_backward(blocks, block_cols, residual, NBC)
    grad_gram = gram_of(gradient)
    direction = gradient
    for iteration in range(ITERS):
        image = apply_forward(blocks, block_cols, direction)
        image_gram = gram_of(image)
        step_size = chol_solve(image_gram, grad_gram)
        solution = solution + jnp.dot(step_size.T, direction, precision=lax.Precision.HIGHEST)
        residual = residual - jnp.dot(step_size.T, image, precision=lax.Precision.HIGHEST)
        if iteration + 1 < ITERS:
            gradient = apply_backward(blocks, block_cols, residual, NBC)
            new_gram = gram_of(gradient)
            mix = chol_solve(grad_gram, new_gram)
            direction = gradient + jnp.dot(mix.T, direction, precision=lax.Precision.HIGHEST)
            grad_gram = new_gram
    return (solution, residual)
```

```python
import functools

import jax
import jax.numpy as jnp
from jax import lax
from jax.experimental import pallas as pl
from jax.experimental.pallas import tpu as pltpu
from jax.sharding import PartitionSpec as P

MESH = pl.DeviceIdType.MESH
F32 = jnp.float32
BF16 = jnp.bfloat16
ITERS = 3
CBD = 8
N = 32
B = 128
STEP_ROWS = 8
MIB = 2**20


def dot(a, b, ca, cb, precision=None):
    return lax.dot_general(
        a, b, (((ca,), (cb,)), ((), ())), precision=precision, preferred_element_type=F32
    )


def exact(a, b, ca=1, cb=0):
    return dot(a, b, ca, cb, lax.Precision.HIGHEST)


def split(x):
    hi = x.astype(BF16)
    lo = (x - hi.astype(F32)).astype(BF16)
    return hi, lo


def stacked(x):
    hi, lo = split(x)
    return jnp.concatenate([hi, lo], axis=0)


def local_kernel(forward, backward, earlier, cols, *refs):
    refs = list(refs)
    blocks = refs.pop(0)
    vec = refs.pop(0)
    before = [refs.pop(0) for _ in range(earlier)]
    image_out = refs.pop(0) if forward else None
    gram_out = refs.pop(0) if forward else None
    sums = refs.pop(0) if backward else None
    parts = refs.pop(0) if forward else None
    gram_acc = refs.pop(0) if forward else None
    step = pl.program_id(0)

    @pl.when(step == 0)
    def _():
        if backward:
            sums[...] = jnp.zeros_like(sums)
        if forward:
            gram_acc[...] = jnp.zeros_like(gram_acc)

            def cut(c, carry):
                hi, lo = split(vec[c])
                parts[c, 0:N, :] = hi
                parts[c, N : 2 * N, :] = lo
                return carry

            lax.fori_loop(0, vec.shape[0], cut, 0, unroll=4)

    for i in range(STEP_ROWS):
        base = (step * STEP_ROWS + i) * 4
        at = slice(i * B, (i + 1) * B)
        tiles = [stacked(blocks[i, k]) for k in range(4)]
        if forward:
            picked = jnp.concatenate([parts[cols[base + k]] for k in range(4)], axis=1)
            quad = dot(picked, jnp.concatenate(tiles, axis=1), 1, 1)
            quad = quad[:N] + quad[N:]
            image = quad[:, :B] + quad[:, B:]
            image_out[:, at] = image
        else:
            image = vec[:, at]
        both = stacked(image)
        if forward:
            others = [both] + [stacked(e[:, at]) for e in before]
            gram_acc[:, : 2 * N * len(others)] += dot(
                both, jnp.concatenate(others, axis=0), 1, 1
            )
        if backward:
            wide = jnp.concatenate([both, both], axis=1)
            piece = dot(wide, jnp.concatenate(tiles, axis=1), 1, 0)
            piece = piece[:N] + piece[N:]
            for k in range(4):
                c = cols[base + k]
                sums[c] += piece[:, k * B : (k + 1) * B]

    if forward:

        @pl.when(step == pl.num_programs(0) - 1)
        def _():
            gram_out[...] = jnp.zeros_like(gram_out)
            for j in range(earlier + 1):
                q = gram_acc[:, 2 * N * j : 2 * N * (j + 1)]
                q = q[:N] + q[N:]
                gram_out[:, N * (j + 1) : N * (j + 2)] = q[:, :N] + q[:, N:]


def local_pass(forward, backward, cols, blocks, vec, before, group):
    rows = blocks.shape[0]
    width = STEP_ROWS * B
    strip = pl.BlockSpec((N, width), lambda s, c: (0, s))
    whole = pl.BlockSpec((group, N, B), lambda s, c: (0, 0, 0))
    outs, out_specs, scratch = [], [], []
    if forward:
        outs += [jax.ShapeDtypeStruct((N, rows * B), F32), jax.ShapeDtypeStruct((N, B), F32)]
        out_specs += [strip, pl.BlockSpec((N, B), lambda s, c: (0, 0))]
        scratch += [pltpu.VMEM((group, 2 * N, B), BF16), pltpu.VMEM((2 * N, 2 * B), F32)]
    if backward:
        outs += [jax.ShapeDtypeStruct((group, N, B), F32)]
        out_specs += [whole]
    return pl.pallas_call(
        functools.partial(local_kernel, forward, backward, len(before)),
        grid_spec=pltpu.PrefetchScalarGridSpec(
            num_scalar_prefetch=1,
            grid=(rows // STEP_ROWS,),
            in_specs=[
                pl.BlockSpec((STEP_ROWS, 4, B, B), lambda s, c: (s, 0, 0, 0)),
                whole if forward else strip,
            ]
            + [strip] * len(before),
            out_specs=out_specs,
            scratch_shapes=scratch,
        ),
        out_shape=outs,
        compiler_params=pltpu.CompilerParams(vmem_limit_bytes=48 * MIB),
    )(cols, blocks, vec, *before)


def spd_solve(matrix, right):
    table = jnp.concatenate([matrix, right], axis=1)
    row_id = lax.broadcasted_iota(jnp.int32, table.shape, 0)
    for k in range(N):
        row = table[k : k + 1, :] / table[k : k + 1, k : k + 1]
        table = jnp.where(row_id == k, row, table - table[:, k : k + 1] * row)
    return table[:, N : 2 * N]


class Traffic:
    def __init__(self, send_sem, recv_sem):
        self.send_sem, self.recv_sem = send_sem, recv_sem
        self.sent = []

    def send(self, slot, src, dst, device):
        copy = pltpu.make_async_remote_copy(
            src_ref=src,
            dst_ref=dst,
            send_sem=self.send_sem.at[slot],
            recv_sem=self.recv_sem.at[slot],
            device_id=device,
            device_id_type=MESH,
        )
        copy.start()
        self.sent.append(copy)
        return copy

    def finish(self):
        for copy in self.sent:
            copy.wait_send()


OFFSETS = (2, 3, 1, 0)


def places(n_x):
    row = lax.axis_index("row")
    col = lax.axis_index("col")
    z, x = row // n_x, lax.rem(row, n_x)

    def along_x(d):
        return (z * n_x + lax.rem(x + d, n_x), col)

    def along_z(d):
        return (lax.rem(z + d, 4) * n_x + x, col)

    return row, col, z, x, along_x, along_z


def reduce_scatter_start(work, z, x, along_x, along_z, r1, tr):
    cps = {}
    for u in range(4):
        for h in range(2):
            pa, pb, ring = (x, z, along_x) if h == 0 else (z, x, along_z)
            tb = lax.rem(pb + OFFSETS[u], 4)

            def src(ta, s, h=h, tb=tb):
                ta = lax.rem(ta, 4)
                return work(h, ta, tb, s)

            base = (h * 4 + u) * 6
            for idx, ta, s, d in ((0, pa + 2, 0, 1), (1, pa + 2, 1, 3), (2, pa + 1, 1, 1), (3, pa + 3, 0, 3)):
                cps[h, u, idx] = tr.send(base + idx, src(ta, s), r1.at[h, u, idx], ring(d))
    return cps


def reduce_scatter_rest(work, z, x, along_x, along_z, r1, p1, r2, tr, cps, hook):
    c2 = {}
    halves = ((x, z, along_x, along_z), (z, x, along_z, along_x))

    def pass_on(u, h):
        pa, pb, ring, _ = halves[h]
        tb = lax.rem(pb + OFFSETS[u], 4)
        base = (h * 4 + u) * 6
        cps[h, u, 0].wait_recv()
        r1[h, u, 0] += work(h, lax.rem(pa + 1, 4), tb, 0)[...]
        cps[h, u, 4] = tr.send(base + 4, r1.at[h, u, 0], r1.at[h, u, 4], ring(1))
        cps[h, u, 1].wait_recv()
        r1[h, u, 1] += work(h, lax.rem(pa + 3, 4), tb, 1)[...]
        cps[h, u, 5] = tr.send(base + 5, r1.at[h, u, 1], r1.at[h, u, 5], ring(3))

    def close(u, h):
        pa, pb, _, ring = halves[h]
        tb = lax.rem(pb + OFFSETS[u], 4)
        base = 48 + h * 6
        for idx in (2, 3, 4, 5):
            cps[h, u, idx].wait_recv()
        p1[h, u, 0:2] = work(h, pa, tb, 0)[...] + (r1[h, u, 3] + r1[h, u, 4])
        p1[h, u, 2:4] = work(h, pa, tb, 1)[...] + (r1[h, u, 2] + r1[h, u, 5])
        if u == 0:
            c2[h, 0] = tr.send(base + 0, p1.at[h, 0, pl.ds(0, 2)], r2.at[h, 0], ring(1))
            c2[h, 1] = tr.send(base + 1, p1.at[h, 0, pl.ds(2, 2)], r2.at[h, 1], ring(3))
        if u == 1:
            c2[h, 3] = tr.send(base + 3, p1.at[h, 1, pl.ds(0, 2)], r2.at[h, 3], ring(3))
            c2[h, 1].wait_recv()
            r2[h, 1] += p1[h, 1, 2:4]
            c2[h, 5] = tr.send(base + 5, r2.at[h, 1], r2.at[h, 5], ring(3))
        if u == 2:
            c2[h, 2] = tr.send(base + 2, p1.at[h, 2, pl.ds(2, 2)], r2.at[h, 2], ring(1))
            c2[h, 0].wait_recv()
            r2[h, 0] += p1[h, 2, 0:2]
            c2[h, 4] = tr.send(base + 4, r2.at[h, 0], r2.at[h, 4], ring(1))

    for u in range(5):
        if u < 4:
            for h in range(2):
                pass_on(u, h)
        if u >= 1:
            for h in range(2):
                close(u - 1, h)
        hook(u)
    own = []
    for h in range(2):
        for idx in (2, 3, 4, 5):
            c2[h, idx].wait_recv()
        first = p1[h, 3, 0:2] + (r2[h, 3] + r2[h, 4])
        second = p1[h, 3, 2:4] + (r2[h, 2] + r2[h, 5])
        own += [first[0], first[1], second[0], second[1]]
    return jnp.concatenate(own, axis=1)


def gather_all(place, z, x, along_x, along_z, tr, base0):
    halves = ((x, z, along_x, along_z), (z, x, along_z, along_x))
    c1, c2 = {}, {}
    order = (0, 3, 1, 2)

    def send1(h, idx):
        pa, pb, _, ring = halves[h]
        off, s, d = ((0, None, 1), (0, None, 3), (3, 0, 1), (1, 1, 3))[idx]
        ref = place(h, pa, lax.rem(pb + off, 4), s)
        c1[h, idx] = tr.send(base0 + h * 4 + idx, ref, ref, ring(d))

    def send2(h, v, idx):
        pa, pb, ring, _ = halves[h]
        tb = lax.rem(pb + order[v], 4)
        off, s, d = ((0, None, 1), (0, None, 3), (3, 0, 1), (1, 1, 3))[idx]
        ref = place(h, lax.rem(pa + off, 4), tb, s)
        c2[h, v, idx] = tr.send(base0 + 8 + (h * 4 + v) * 4 + idx, ref, ref, ring(d))

    both = range(2)
    for h in both:
        send1(h, 0)
        send1(h, 1)
    for h in both:
        send2(h, 0, 0)
        send2(h, 0, 1)
    for h in both:
        c1[h, 0].wait_recv()
        send1(h, 2)
        send2(h, 1, 0)
        send2(h, 1, 1)
        c1[h, 1].wait_recv()
        send1(h, 3)
        send2(h, 2, 0)
        send2(h, 2, 1)
    for v in range(4):
        for h in both:
            if v == 1:
                c1[h, 2].wait_recv()
                c1[h, 3].wait_recv()
                send2(h, 3, 0)
                send2(h, 3, 1)
            c2[h, v, 0].wait_recv()
            send2(h, v, 2)
            c2[h, v, 1].wait_recv()
            send2(h, v, 3)
    for v in range(4):
        for h in both:
            c2[h, v, 2].wait_recv()
            c2[h, v, 3].wait_recv()


RS_SLOTS = 60
AG_SLOTS = 40


class GramSum:
    def __init__(self, row, col, n_row, n_col, tr, slot0, box1, box2):
        self.row, self.col, self.n_row, self.n_col = row, col, n_row, n_col
        self.tr, self.slot0, self.box1, self.box2 = tr, slot0, box1, box2

    def first(self, tile):
        self.box1[self.col] = tile
        self.c1 = []
        for d in range(1, self.n_col):
            ref = self.box1.at[self.col]
            to = (self.row, lax.rem(self.col + d, self.n_col))
            self.c1.append(self.tr.send(self.slot0 + d - 1, ref, ref, to))

    def second(self):
        for c in self.c1:
            c.wait_recv()
        total = self.box1[0]
        for i in range(1, self.n_col):
            total = total + self.box1[i]
        self.box2[self.row] = total
        self.c2 = []
        for d in range(1, self.n_row):
            ref = self.box2.at[self.row]
            to = (lax.rem(self.row + d, self.n_row), self.col)
            self.c2.append(self.tr.send(self.slot0 + self.n_col - 1 + d - 1, ref, ref, to))

    def total(self):
        for c in self.c2:
            c.wait_recv()
        total = self.box2[0]
        for i in range(1, self.n_row):
            total = total + self.box2[i]
        return total


def meet(row, col, n_row, n_col, along_x, along_z, grams):
    barrier = pltpu.get_barrier_semaphore()
    if grams:
        who = [(row, lax.rem(col + d, n_col)) for d in range(1, n_col)]
        who += [(lax.rem(row + d, n_row), col) for d in range(1, n_row)]
    else:
        who = [along_x(1), along_x(3), along_z(1), along_z(3)]
    for device in who:
        pl.semaphore_signal(barrier, inc=1, device_id=device, device_id_type=MESH)
    pl.semaphore_wait(barrier, len(who))


GG, IG, MIX1, STEP0, STEP1 = range(5)


def small_solves(k, total, state):
    gg = total[:, 0:N]
    image_gram = total[:, N : 2 * N]
    mix = None
    if k >= 2:
        mix = spd_solve(state[GG], gg)
        cross = total[:, 2 * N : 3 * N]
        if k == 3:
            cross = cross + exact(total[:, 3 * N : 4 * N], state[MIX1])
        mixed = exact(cross, mix)
        image_gram = image_gram + (mixed + mixed.T) + exact(mix, exact(state[IG], mix), 0, 0)
    step = spd_solve(image_gram, gg)
    return gg, image_gram, mix, step


def exchange_kernel(k, n_row, n_col, *refs):
    refs = list(refs)
    sums = refs.pop(0)
    if k:
        gram_in, tile_in, grad_in, state_in = (refs.pop(0) for _ in range(4))
    if k >= 2:
        conj_in = refs.pop(0)
    vec, grad_out, tile_out = (refs.pop(0) for _ in range(3))
    if k:
        conj_out, state_out = refs.pop(0), refs.pop(0)
    r1, p1, r2, send_sem, recv_sem = (refs.pop(0) for _ in range(5))
    if k:
        box1, box2 = refs.pop(0), refs.pop(0)
    row, col, z, x, along_x, along_z = places(n_row // 4)
    tr = Traffic(send_sem, recv_sem)
    meet(row, col, n_row, n_col, along_x, along_z, k > 0)

    def work(h, ta, tb, s):
        zz, xx = (tb, ta) if h == 0 else (ta, tb)
        return sums.at[zz, xx, h, pl.ds(2 * s, 2)]

    def place(h, ta, tb, s):
        zz, xx = (tb, ta) if h == 0 else (ta, tb)
        return vec.at[zz, xx, h] if s is None else vec.at[zz, xx, h, pl.ds(2 * s, 2)]

    if k:
        grams = GramSum(row, col, n_row, n_col, tr, RS_SLOTS + AG_SLOTS, box1, box2)
        grams.first(gram_in[...] + tile_in[...])
    cps = reduce_scatter_start(work, z, x, along_x, along_z, r1, tr)
    found = []

    def hook(u):
        if k and u == 0:
            grams.second()
        if k and u == 2:
            found.extend(small_solves(k, grams.total(), state_in))

    fresh = reduce_scatter_rest(work, z, x, along_x, along_z, r1, p1, r2, tr, cps, hook)
    if k == 0:
        grad = fresh
    else:
        gg, image_gram, mix, step = found
        conj = fresh if k == 1 else fresh + exact(mix, conj_in[...], 0, 0)
        grad = grad_in[...] - exact(step, conj, 0, 0)
        conj_out[...] = conj
        state_out[GG] = gg
        state_out[IG] = image_gram
        state_out[MIX1] = mix if k == 2 else jnp.zeros((N, N), F32)
        state_out[STEP0] = step if k == 1 else state_in[STEP0]
        state_out[STEP1] = step if k == 2 else jnp.zeros((N, N), F32)
    for h in range(2):
        for j in range(4):
            at = (4 * h + j) * B
            vec[z, x, h, j] = grad[:, at : at + B]
    grad_out[...] = grad
    tile_out[...] = jnp.zeros_like(tile_out)
    tile_out[:, 0:N] = exact(grad, grad, 1, 1)
    gather_all(place, z, x, along_x, along_z, tr, RS_SLOTS)
    tr.finish()


def exchange(k, n_row, n_col, sums, more):
    shape = (4, n_row // 4, 2, CBD // 2, N, B)
    vmem = pl.BlockSpec(memory_space=pltpu.VMEM)
    width = CBD * B
    outs = [
        jax.ShapeDtypeStruct(shape, F32),
        jax.ShapeDtypeStruct((N, width), F32),
        jax.ShapeDtypeStruct((N, B), F32),
    ]
    slots = RS_SLOTS + AG_SLOTS
    scratch = [
        pltpu.VMEM((2, 4, 6, 2, N, B), F32),
        pltpu.VMEM((2, 4, 4, N, B), F32),
        pltpu.VMEM((2, 6, 2, N, B), F32),
    ]
    boxes = []
    if k:
        outs += [jax.ShapeDtypeStruct((N, width), F32), jax.ShapeDtypeStruct((5, N, N), F32)]
        slots += n_row - 1 + n_col - 1
        boxes = [pltpu.VMEM((n_col, N, B), F32), pltpu.VMEM((n_row, N, B), F32)]
    return pl.pallas_call(
        functools.partial(exchange_kernel, k, n_row, n_col),
        out_shape=outs,
        in_specs=[vmem] * (1 + len(more)),
        out_specs=[vmem] * len(outs),
        scratch_shapes=scratch
        + [pltpu.SemaphoreType.DMA((slots,)), pltpu.SemaphoreType.DMA((slots,))]
        + boxes,
        compiler_params=pltpu.CompilerParams(
            collective_id=k, has_side_effects=True, vmem_limit_bytes=48 * MIB
        ),
    )(sums.reshape(shape), *more)


def coefficient_kernel(n_row, n_col, gram_in, tile_in, state_in, coef, send_sem, recv_sem, box1, box2):
    row, col, z, x, along_x, along_z = places(n_row // 4)
    tr = Traffic(send_sem, recv_sem)
    meet(row, col, n_row, n_col, along_x, along_z, True)
    grams = GramSum(row, col, n_row, n_col, tr, 0, box1, box2)
    grams.first(gram_in[...] + tile_in[...])
    grams.second()
    total = grams.total()
    _, _, mix2, step2 = small_solves(3, total, state_in)
    e1 = state_in[STEP1] + exact(mix2, step2)
    coef[0:N, :] = state_in[STEP0] + exact(state_in[MIX1], e1)
    coef[N : 2 * N, :] = e1
    coef[2 * N : 3 * N, :] = step2
    tr.finish()


def coefficients(n_row, n_col, gram, tile, state):
    vmem = pl.BlockSpec(memory_space=pltpu.VMEM)
    slots = n_row + n_col - 2
    return pl.pallas_call(
        functools.partial(coefficient_kernel, n_row, n_col),
        out_shape=jax.ShapeDtypeStruct((3 * N, N), F32),
        in_specs=[vmem] * 3,
        out_specs=vmem,
        scratch_shapes=[
            pltpu.SemaphoreType.DMA((slots,)),
            pltpu.SemaphoreType.DMA((slots,)),
            pltpu.VMEM((n_col, N, B), F32),
            pltpu.VMEM((n_row, N, B), F32),
        ],
        compiler_params=pltpu.CompilerParams(collective_id=3, has_side_effects=True),
    )(gram, tile, state)


def final_kernel(coef, t, i0, i1, i2, g0, g1, g2, sol, res):
    weights = coef[...]

    @pl.when(pl.program_id(0) == 0)
    def _():
        sol[...] = exact(weights, jnp.concatenate([g0[...], g1[...], g2[...]], axis=0), 0, 0)

    res[...] = t[...] - exact(weights, jnp.concatenate([i0[...], i1[...], i2[...]], axis=0), 0, 0)


def finish(coef, targets, images, grads):
    width = 1024
    strip = pl.BlockSpec((N, width), lambda s: (0, s))
    fixed = pl.BlockSpec((N, CBD * B), lambda s: (0, 0))
    return pl.pallas_call(
        final_kernel,
        grid=(targets.shape[1] // width,),
        out_shape=[
            jax.ShapeDtypeStruct((N, CBD * B), F32),
            jax.ShapeDtypeStruct(targets.shape, F32),
        ],
        in_specs=[pl.BlockSpec((3 * N, N), lambda s: (0, 0))] + [strip] * 4 + [fixed] * 3,
        out_specs=[fixed, strip],
    )(coef, targets, *images, *grads)


def body(blocks, block_cols, targets):
    n_row = lax.axis_size("row")
    n_col = lax.axis_size("col")
    group = CBD * n_row
    flat = block_cols.reshape(-1)
    cols = flat // (CBD * n_col) * CBD + lax.rem(flat, CBD)

    (sums,) = local_pass(False, True, cols, blocks, targets, [], group)
    vec, grad, tile = exchange(0, n_row, n_col, sums, [])
    grads, images = [grad], []
    state = jnp.zeros((5, N, N), F32)
    conj = None
    for k in range(1, ITERS + 1):
        last = k == ITERS
        made = local_pass(True, not last, cols, blocks, vec.reshape(group, N, B), images[::-1], group)
        images.append(made[0])
        gram = made[1]
        if last:
            coef = coefficients(n_row, n_col, gram, tile, state)
        else:
            more = [gram, tile, grad, state] + ([conj] if k >= 2 else [])
            vec, grad, tile, conj, state = exchange(k, n_row, n_col, made[2], more)
            grads.append(grad)
    return tuple(finish(coef, targets, images, grads))


def solution(mesh):
    placed = (P(("row", "col"), None, None, None), P(("row", "col"), None), P(None, ("row", "col")))
    return jax.shard_map(
        body,
        mesh=mesh,
        in_specs=placed,
        out_specs=(P(None, ("row", "col")), P(None, ("row", "col"))),
        check_vma=False,
    )
```

```python
import functools

import jax
import jax.numpy as jnp
from jax import lax
from jax.experimental import pallas as pl
from jax.experimental.pallas import tpu as pltpu
from jax.sharding import PartitionSpec as P

MESH = pl.DeviceIdType.MESH
F32 = jnp.float32
BF16 = jnp.bfloat16
ITERS = 3
CBD = 8
N = 32
B = 128
STEP_ROWS = 8
MIB = 2**20


def dot(a, b, ca, cb, precision=None):
    return lax.dot_general(
        a, b, (((ca,), (cb,)), ((), ())), precision=precision, preferred_element_type=F32
    )


def exact(a, b, ca=1, cb=0):
    return dot(a, b, ca, cb, lax.Precision.HIGHEST)


def split(x):
    hi = x.astype(BF16)
    lo = (x - hi.astype(F32)).astype(BF16)
    return hi, lo


def stacked(x):
    hi, lo = split(x)
    return jnp.concatenate([hi, lo], axis=0)


def pack(square):
    return jnp.concatenate([square[8 * g : 8 * g + 8] for g in range(4)], axis=1)


def unpack(tile):
    return jnp.concatenate([tile[:, N * g : N * g + N] for g in range(4)], axis=0)


def fold(square):
    half = square[:N] + square[N:]
    return half[:, :N] + half[:, N:]


def add_pieces(cols, base, both, block, sums):
    piece = dot(jnp.concatenate([both, both], axis=1), block, 1, 0)
    piece = piece[:N] + piece[N:]
    for k in range(4):
        c = cols[base + k]
        sums[c] += piece[:, k * B : (k + 1) * B]


def first_kernel(cols, blocks, targets, across_out, down_out, sums):
    step = pl.program_id(0)

    @pl.when(step == 0)
    def _():
        sums[...] = jnp.zeros_like(sums)

    for i in range(STEP_ROWS):
        his, los = [], []
        for k in range(4):
            hi, lo = split(blocks[i, k])
            his.append(hi)
            los.append(lo)
            down_out[i, k * B : (k + 1) * B, 0:B] = hi.T
            down_out[i, k * B : (k + 1) * B, B : 2 * B] = lo.T
        across = jnp.concatenate([jnp.concatenate(his, axis=1), jnp.concatenate(los, axis=1)], axis=0)
        across_out[i] = across
        both = stacked(targets[:, i * B : (i + 1) * B])
        add_pieces(cols, (step * STEP_ROWS + i) * 4, both, across, sums)


def first_pass(cols, blocks, targets, group):
    rows = blocks.shape[0]
    return pl.pallas_call(
        first_kernel,
        grid_spec=pltpu.PrefetchScalarGridSpec(
            num_scalar_prefetch=1,
            grid=(rows // STEP_ROWS,),
            in_specs=[
                pl.BlockSpec((STEP_ROWS, 4, B, B), lambda s, c: (s, 0, 0, 0)),
                pl.BlockSpec((N, STEP_ROWS * B), lambda s, c: (0, s)),
            ],
            out_specs=[
                pl.BlockSpec((STEP_ROWS, 2 * B, 4 * B), lambda s, c: (s, 0, 0)),
                pl.BlockSpec((STEP_ROWS, 4 * B, 2 * B), lambda s, c: (s, 0, 0)),
                pl.BlockSpec((group, N, B), lambda s, c: (0, 0, 0)),
            ],
        ),
        out_shape=[
            jax.ShapeDtypeStruct((rows, 2 * B, 4 * B), BF16),
            jax.ShapeDtypeStruct((rows, 4 * B, 2 * B), BF16),
            jax.ShapeDtypeStruct((group, N, B), F32),
        ],
        compiler_params=pltpu.CompilerParams(vmem_limit_bytes=48 * MIB),
    )(cols, blocks, targets)


def pass_kernel(k, backward, cols, *refs):
    refs = list(refs)
    down = refs.pop(0)
    across = refs.pop(0) if backward else None
    vec = refs.pop(0)
    before = [refs.pop(0) for _ in range(k)]
    state = [refs.pop(0) for _ in range(k)]
    gram_before = refs.pop(0) if k else None
    image_out, gram_out, tile_out = (refs.pop(0) for _ in range(3))
    sums = refs.pop(0) if backward else None
    parts, gram_acc = refs
    step = pl.program_id(0)

    @pl.when(step == 0)
    def _():
        if backward:
            sums[...] = jnp.zeros_like(sums)
        gram_acc[...] = jnp.zeros_like(gram_acc)

        def cut(c, carry):
            parts[c] = stacked(vec[c])
            return carry

        lax.fori_loop(0, vec.shape[0], cut, 0, unroll=8)

    for i in range(STEP_ROWS):
        base = (step * STEP_ROWS + i) * 4
        picked = jnp.concatenate([parts[cols[base + j]] for j in range(4)], axis=1)
        quad = dot(picked, down[i], 1, 0)
        quad = quad[:N] + quad[N:]
        both = stacked(quad[:, :B] + quad[:, B:])
        image_out[:, i * B : (i + 1) * B] = both
        if backward:
            add_pieces(cols, base, both, across[i], sums)
    mine = image_out[...]
    for j, other in enumerate([mine] + [e[...] for e in before]):
        gram_acc[j] += dot(mine, other, 1, 1)

    @pl.when(step == pl.num_programs(0) - 1)
    def _():
        gram = fold(gram_acc[0])
        if k:
            mix = state[0][MIX]
            cross = fold(gram_acc[1])
            if k == 2:
                cross = cross + exact(fold(gram_acc[2]), state[1][MIX])
            mixed = exact(cross, mix)
            gram = gram + (mixed + mixed.T) + exact(mix, exact(gram_before[...], mix), 0, 0)
        gram_out[...] = gram
        tile_out[...] = pack(gram)


def local_pass(k, backward, cols, down, across, vec, images, states, gram, group):
    rows = down.shape[0]
    strip = pl.BlockSpec((2 * N, STEP_ROWS * B), lambda s, c: (0, s))
    whole = pl.BlockSpec((group, N, B), lambda s, c: (0, 0, 0))
    square = pl.BlockSpec((N, N), lambda s, c: (0, 0))
    three = pl.BlockSpec((3, N, N), lambda s, c: (0, 0, 0))
    args = [down] + ([across] if backward else []) + [vec]
    in_specs = [pl.BlockSpec((STEP_ROWS, 4 * B, 2 * B), lambda s, c: (s, 0, 0))]
    if backward:
        in_specs += [pl.BlockSpec((STEP_ROWS, 2 * B, 4 * B), lambda s, c: (s, 0, 0))]
    in_specs += [whole]
    if k:
        args += images[::-1] + states[::-1][:k] + [gram]
        in_specs += [strip] * k + [three] * k + [square]
    outs = [
        jax.ShapeDtypeStruct((2 * N, rows * B), BF16),
        jax.ShapeDtypeStruct((N, N), F32),
        jax.ShapeDtypeStruct((8, B), F32),
    ]
    out_specs = [strip, square, pl.BlockSpec((8, B), lambda s, c: (0, 0))]
    if backward:
        outs += [jax.ShapeDtypeStruct((group, N, B), F32)]
        out_specs += [whole]
    return pl.pallas_call(
        functools.partial(pass_kernel, k, backward),
        grid_spec=pltpu.PrefetchScalarGridSpec(
            num_scalar_prefetch=1,
            grid=(rows // STEP_ROWS,),
            in_specs=in_specs,
            out_specs=out_specs,
            scratch_shapes=[
                pltpu.VMEM((group, 2 * N, B), BF16),
                pltpu.VMEM((k + 1, 2 * N, 2 * N), F32),
            ],
        ),
        out_shape=outs,
        compiler_params=pltpu.CompilerParams(vmem_limit_bytes=48 * MIB),
    )(cols, *args)


def spd_solve(matrix, right):
    table = jnp.concatenate([matrix, right], axis=1)
    wide = (8, 2 * N)
    parts = [table[8 * g : 8 * g + 8] for g in range(4)]
    sub = lax.broadcasted_iota(jnp.int32, wide, 0)

    def lanes(group, b):
        return jnp.broadcast_to(group[:, b : b + 1], wide)

    def rows(group, a):
        return jnp.broadcast_to(group[a : a + 1], wide)

    for g in range(4):
        mine = parts[g]
        pivots = [lanes(mine, 8 * g + b) for b in range(8)]
        factors = [[lanes(parts[h], 8 * g + b) for b in range(8)] if h != g else None for h in range(4)]
        for a in range(8):
            inverse = 1.0 / rows(pivots[a], a)
            here = sub == a
            factor = pivots[a]
            for b in range(a + 1, 8):
                scaled = rows(pivots[b], a) * inverse
                pivots[b] = jnp.where(here, scaled, pivots[b] - factor * scaled)
            scaled = rows(mine, a) * inverse
            mine = jnp.where(here, scaled, mine - factor * scaled)
        parts[g] = mine
        for h in range(4):
            if h != g:
                for b in range(8):
                    parts[h] = parts[h] - factors[h][b] * rows(mine, b)
    return jnp.concatenate(parts, axis=0)[:, N : 2 * N]


def apply_t(square, both):
    hi, lo = split(square.T)
    left = jnp.concatenate([jnp.concatenate([hi, hi], axis=1), jnp.concatenate([lo, lo], axis=1)], axis=0)
    out = dot(left, both, 1, 0)
    return out[:N] + out[N:]


class Traffic:
    def __init__(self, send_sem, recv_sem):
        self.send_sem, self.recv_sem = send_sem, recv_sem
        self.sent = []

    def send(self, slot, src, dst, device):
        copy = pltpu.make_async_remote_copy(
            src_ref=src,
            dst_ref=dst,
            send_sem=self.send_sem.at[slot],
            recv_sem=self.recv_sem.at[slot],
            device_id=device,
            device_id_type=MESH,
        )
        copy.start()
        self.sent.append(copy)
        return copy

    def finish(self):
        for copy in self.sent:
            copy.wait_send()


OFFSETS = (2, 3, 1, 0)


def places(n_x):
    row = lax.axis_index("row")
    col = lax.axis_index("col")
    z, x = row // n_x, lax.rem(row, n_x)

    def along_x(d):
        return (z * n_x + lax.rem(x + d, n_x), col)

    def along_z(d):
        return (lax.rem(z + d, 4) * n_x + x, col)

    return row, col, z, x, along_x, along_z


def reduce_scatter_start(work, z, x, along_x, along_z, r1, tr):
    cps = {}
    for u in range(4):
        for h in range(2):
            pa, pb, ring = (x, z, along_x) if h == 0 else (z, x, along_z)
            tb = lax.rem(pb + OFFSETS[u], 4)

            def src(ta, s, h=h, tb=tb):
                ta = lax.rem(ta, 4)
                return work(h, ta, tb, s)

            base = (h * 4 + u) * 6
            for idx, ta, s, d in ((0, pa + 2, 0, 1), (1, pa + 2, 1, 3), (2, pa + 1, 1, 1), (3, pa + 3, 0, 3)):
                cps[h, u, idx] = tr.send(base + idx, src(ta, s), r1.at[h, u, idx], ring(d))
    return cps


def reduce_scatter_rest(work, z, x, along_x, along_z, r1, p1, r2, tr, cps, hook):
    c2 = {}
    halves = ((x, z, along_x, along_z), (z, x, along_z, along_x))

    def pass_on(u, h):
        pa, pb, ring, _ = halves[h]
        tb = lax.rem(pb + OFFSETS[u], 4)
        base = (h * 4 + u) * 6
        cps[h, u, 0].wait_recv()
        r1[h, u, 0] += work(h, lax.rem(pa + 1, 4), tb, 0)[...]
        cps[h, u, 4] = tr.send(base + 4, r1.at[h, u, 0], r1.at[h, u, 4], ring(1))
        cps[h, u, 1].wait_recv()
        r1[h, u, 1] += work(h, lax.rem(pa + 3, 4), tb, 1)[...]
        cps[h, u, 5] = tr.send(base + 5, r1.at[h, u, 1], r1.at[h, u, 5], ring(3))

    def close(u, h):
        pa, pb, _, ring = halves[h]
        tb = lax.rem(pb + OFFSETS[u], 4)
        base = 48 + h * 6
        for idx in (2, 3, 4, 5):
            cps[h, u, idx].wait_recv()
        p1[h, u, 0:2] = work(h, pa, tb, 0)[...] + (r1[h, u, 3] + r1[h, u, 4])
        p1[h, u, 2:4] = work(h, pa, tb, 1)[...] + (r1[h, u, 2] + r1[h, u, 5])
        if u == 0:
            c2[h, 0] = tr.send(base + 0, p1.at[h, 0, pl.ds(0, 2)], r2.at[h, 0], ring(1))
            c2[h, 1] = tr.send(base + 1, p1.at[h, 0, pl.ds(2, 2)], r2.at[h, 1], ring(3))
        if u == 1:
            c2[h, 3] = tr.send(base + 3, p1.at[h, 1, pl.ds(0, 2)], r2.at[h, 3], ring(3))
            c2[h, 1].wait_recv()
            r2[h, 1] += p1[h, 1, 2:4]
            c2[h, 5] = tr.send(base + 5, r2.at[h, 1], r2.at[h, 5], ring(3))
        if u == 2:
            c2[h, 2] = tr.send(base + 2, p1.at[h, 2, pl.ds(2, 2)], r2.at[h, 2], ring(1))
            c2[h, 0].wait_recv()
            r2[h, 0] += p1[h, 2, 0:2]
            c2[h, 4] = tr.send(base + 4, r2.at[h, 0], r2.at[h, 4], ring(1))

    for u in range(5):
        if u < 4:
            for h in range(2):
                pass_on(u, h)
        if u >= 1:
            for h in range(2):
                close(u - 1, h)
        hook(u)
    own = []
    for h in range(2):
        for idx in (2, 3, 4, 5):
            c2[h, idx].wait_recv()
        first = p1[h, 3, 0:2] + (r2[h, 3] + r2[h, 4])
        second = p1[h, 3, 2:4] + (r2[h, 2] + r2[h, 5])
        own += [first[0], first[1], second[0], second[1]]
    return jnp.concatenate(own, axis=1)


def gather_all(place, z, x, along_x, along_z, tr, base0, hook):
    halves = ((x, z, along_x, along_z), (z, x, along_z, along_x))
    c1, c2 = {}, {}
    order = (0, 3, 1, 2)

    def send1(h, idx):
        pa, pb, _, ring = halves[h]
        off, s, d = ((0, None, 1), (0, None, 3), (3, 0, 1), (1, 1, 3))[idx]
        ref = place(h, pa, lax.rem(pb + off, 4), s)
        c1[h, idx] = tr.send(base0 + h * 4 + idx, ref, ref, ring(d))

    def send2(h, v, idx):
        pa, pb, ring, _ = halves[h]
        tb = lax.rem(pb + order[v], 4)
        off, s, d = ((0, None, 1), (0, None, 3), (3, 0, 1), (1, 1, 3))[idx]
        ref = place(h, lax.rem(pa + off, 4), tb, s)
        c2[h, v, idx] = tr.send(base0 + 8 + (h * 4 + v) * 4 + idx, ref, ref, ring(d))

    both = range(2)
    for h in both:
        send1(h, 0)
        send1(h, 1)
    for h in both:
        send2(h, 0, 0)
        send2(h, 0, 1)
    for h in both:
        c1[h, 0].wait_recv()
        send1(h, 2)
        send2(h, 1, 0)
        send2(h, 1, 1)
        c1[h, 1].wait_recv()
        send1(h, 3)
        send2(h, 2, 0)
        send2(h, 2, 1)
    for v in range(4):
        for h in both:
            if v == 1:
                c1[h, 2].wait_recv()
                c1[h, 3].wait_recv()
                send2(h, 3, 0)
                send2(h, 3, 1)
            c2[h, v, 0].wait_recv()
            send2(h, v, 2)
            c2[h, v, 1].wait_recv()
            send2(h, v, 3)
        hook(v)
    for v in range(4):
        for h in both:
            c2[h, v, 2].wait_recv()
            c2[h, v, 3].wait_recv()


RS_SLOTS = 60
AG_SLOTS = 40


SUM_SLOTS = 10


def sum_stages(row, col, n_row, n_col):
    n_x, n_y = n_row // 4, n_col // 2
    z, x = row // n_x, lax.rem(row, n_x)
    y, core = col // 2, lax.rem(col, 2)
    return [
        ([(row, y * 2 + 1 - core)], core, 2),
        ([(row, lax.rem(y + d, n_y) * 2 + core) for d in range(1, n_y)], y, n_y),
        ([(z * n_x + lax.rem(x + d, n_x), col) for d in range(1, n_x)], x, n_x),
        ([(lax.rem(z + d, 4) * n_x + x, col) for d in range(1, 4)], z, 4),
    ]


class TileSum:
    def __init__(self, stages, tr, slot, box):
        self.stages, self.tr, self.slot, self.box = stages, tr, slot, box
        self.at, self.open = 0, []

    def put(self, tile):
        peers, me, _ = self.stages[self.at]
        ref = self.box.at[self.at, me]
        self.box[self.at, me] = tile
        self.open = []
        for device in peers:
            self.open.append(self.tr.send(self.slot, ref, ref, device))
            self.slot += 1

    def take(self):
        for c in self.open:
            c.wait_recv()
        size = self.stages[self.at][2]
        total = self.box[self.at, 0]
        for i in range(1, size):
            total = total + self.box[self.at, i]
        self.at += 1
        return total

    def step(self):
        self.put(self.take())


def meet(stages):
    barrier = pltpu.get_barrier_semaphore()
    who = [device for peers, _, _ in stages for device in peers]
    for device in who:
        pl.semaphore_signal(barrier, inc=1, device_id=device, device_id_type=MESH)
    pl.semaphore_wait(barrier, len(who))


GG, MIX, STEP = range(3)


def exchange_kernel(k, n_row, n_col, *refs):
    refs = list(refs)
    sums = refs.pop(0)
    if k:
        tile_in, grad_in, state_in = (refs.pop(0) for _ in range(3))
    conj_in = refs.pop(0) if k >= 2 else None
    vec, grad_out, state_out = (refs.pop(0) for _ in range(3))
    conj_out = refs.pop(0) if k else None
    r1, p1, r2, box, send_sem, recv_sem = refs
    row, col, z, x, along_x, along_z = places(n_row // 4)
    stages = sum_stages(row, col, n_row, n_col)
    tr = Traffic(send_sem, recv_sem)
    meet(stages)

    def work(h, ta, tb, s):
        zz, xx = (tb, ta) if h == 0 else (ta, tb)
        return sums.at[zz, xx, h, pl.ds(2 * s, 2)]

    def place(h, ta, tb, s):
        zz, xx = (tb, ta) if h == 0 else (ta, tb)
        return vec.at[zz, xx, h] if s is None else vec.at[zz, xx, h, pl.ds(2 * s, 2)]

    slots = RS_SLOTS + AG_SLOTS
    if k:
        image_sum = TileSum(stages, tr, slots, box.at[0])
        image_sum.put(tile_in[...])
    cps = reduce_scatter_start(work, z, x, along_x, along_z, r1, tr)
    found = []

    def beside_first(u):
        if k and u < 3:
            image_sum.step()
        if k and u == 3:
            found.append(spd_solve(unpack(image_sum.take()), state_in[GG]))

    fresh = reduce_scatter_rest(work, z, x, along_x, along_z, r1, p1, r2, tr, cps, beside_first)
    if k == 0:
        grad = fresh
    else:
        (step,) = found
        conj = fresh if k == 1 else fresh + apply_t(state_in[MIX], stacked(conj_in[...]))
        grad = grad_in[...] - apply_t(step, stacked(conj))
    for h in range(2):
        for j in range(4):
            at = (4 * h + j) * B
            vec[z, x, h, j] = grad[:, at : at + B]
    grad_sum = TileSum(stages, tr, slots + SUM_SLOTS, box.at[1])

    def beside_second(v):
        if v == 0:
            both = stacked(grad)
            grad_sum.put(pack(fold(dot(both, both, 1, 1))))
            grad_out[...] = grad
            if k:
                conj_out[...] = conj
        else:
            grad_sum.step()

    gather_all(place, z, x, along_x, along_z, tr, RS_SLOTS, beside_second)
    gram = unpack(grad_sum.take())
    state_out[GG] = gram
    state_out[MIX] = spd_solve(state_in[GG], gram) if k else jnp.zeros((N, N), F32)
    state_out[STEP] = step if k else jnp.zeros((N, N), F32)
    tr.finish()


def exchange(k, n_row, n_col, sums, more):
    shape = (4, n_row // 4, 2, CBD // 2, N, B)
    vmem = pl.BlockSpec(memory_space=pltpu.VMEM)
    width = CBD * B
    outs = [
        jax.ShapeDtypeStruct(shape, F32),
        jax.ShapeDtypeStruct((N, width), F32),
        jax.ShapeDtypeStruct((3, N, N), F32),
    ]
    if k:
        outs += [jax.ShapeDtypeStruct((N, width), F32)]
    slots = RS_SLOTS + AG_SLOTS + 2 * SUM_SLOTS
    return pl.pallas_call(
        functools.partial(exchange_kernel, k, n_row, n_col),
        out_shape=outs,
        in_specs=[vmem] * (1 + len(more)),
        out_specs=[vmem] * len(outs),
        scratch_shapes=[
            pltpu.VMEM((2, 4, 6, 2, N, B), F32),
            pltpu.VMEM((2, 4, 4, N, B), F32),
            pltpu.VMEM((2, 6, 2, N, B), F32),
            pltpu.VMEM((2, 4, 4, 8, B), F32),
            pltpu.SemaphoreType.DMA((slots,)),
            pltpu.SemaphoreType.DMA((slots,)),
        ],
        compiler_params=pltpu.CompilerParams(
            collective_id=k, has_side_effects=True, vmem_limit_bytes=48 * MIB
        ),
    )(sums.reshape(shape), *more)


def last_kernel(n_row, n_col, *refs):
    tile_in, s1, s2, t_hbm, i0, i1, i2, g0, g1, g2, sol, res = refs[:12]
    t_mem, i_mem, g_mem, box, send_sem, recv_sem, load_sem = refs[12:]
    loads = [pltpu.make_async_copy(t_hbm, t_mem, load_sem.at[0])]
    for j, (image, grad) in enumerate(((i0, g0), (i1, g1), (i2, g2))):
        loads.append(pltpu.make_async_copy(image, i_mem.at[pl.ds(2 * N * j, 2 * N)], load_sem.at[1 + 2 * j]))
        loads.append(pltpu.make_async_copy(grad, g_mem.at[j], load_sem.at[2 + 2 * j]))
    for copy in loads:
        copy.start()
    row, col = lax.axis_index("row"), lax.axis_index("col")
    stages = sum_stages(row, col, n_row, n_col)
    tr = Traffic(send_sem, recv_sem)
    meet(stages)
    image_sum = TileSum(stages, tr, 0, box)
    image_sum.put(tile_in[...])
    for _ in range(3):
        image_sum.step()
    total = image_sum.take()
    e2 = spd_solve(unpack(total), s2[GG])
    e1 = s2[STEP] + exact(s2[MIX], e2)
    e0 = s1[STEP] + exact(s1[MIX], e1)
    his, los = [], []
    for e in (e0, e1, e2):
        hi, lo = split(e.T)
        his += [hi, hi]
        los += [lo, lo]
    left = jnp.concatenate([jnp.concatenate(his, axis=1), jnp.concatenate(los, axis=1)], axis=0)
    for copy in loads:
        copy.wait()
    right = jnp.concatenate([stacked(g_mem[j]) for j in range(3)], axis=0)
    out = dot(left, right, 1, 0)
    sol[...] = out[:N] + out[N:]
    width = 1024

    def strip(s, carry):
        at = pl.ds(pl.multiple_of(s * width, width), width)
        out = dot(left, i_mem[:, at], 1, 0)
        res[:, at] = t_mem[:, at] - (out[:N] + out[N:])
        return carry

    lax.fori_loop(0, t_mem.shape[1] // width, strip, 0)
    tr.finish()


def last(n_row, n_col, tile, states, targets, images, grads):
    vmem = pl.BlockSpec(memory_space=pltpu.VMEM)
    anywhere = pl.BlockSpec(memory_space=pl.ANY)
    width = CBD * B
    return pl.pallas_call(
        functools.partial(last_kernel, n_row, n_col),
        out_shape=[jax.ShapeDtypeStruct((N, width), F32), jax.ShapeDtypeStruct(targets.shape, F32)],
        in_specs=[vmem] * 3 + [anywhere] * 7,
        out_specs=[vmem] * 2,
        scratch_shapes=[
            pltpu.VMEM(targets.shape, F32),
            pltpu.VMEM((6 * N, targets.shape[1]), BF16),
            pltpu.VMEM((3, N, width), F32),
            pltpu.VMEM((4, 4, 8, B), F32),
            pltpu.SemaphoreType.DMA((SUM_SLOTS,)),
            pltpu.SemaphoreType.DMA((SUM_SLOTS,)),
            pltpu.SemaphoreType.DMA((7,)),
        ],
        compiler_params=pltpu.CompilerParams(
            collective_id=3, has_side_effects=True, vmem_limit_bytes=32 * MIB
        ),
    )(tile, *states, targets, *images, *grads)


def body(blocks, block_cols, targets):
    n_row = lax.axis_size("row")
    n_col = lax.axis_size("col")
    group = CBD * n_row
    flat = block_cols.reshape(-1)
    cols = flat // (CBD * n_col) * CBD + lax.rem(flat, CBD)

    across, down, sums = first_pass(cols, blocks, targets, group)
    vec, grad, state = exchange(0, n_row, n_col, sums, [])
    grads, images, states = [grad], [], [state]
    conj = gram = None
    for k in range(ITERS):
        final = k + 1 == ITERS
        made = local_pass(
            k, not final, cols, down, across, vec.reshape(group, N, B), images, states, gram, group
        )
        images.append(made[0])
        gram, tile = made[1], made[2]
        if not final:
            more = [tile, grad, state] + ([conj] if k else [])
            vec, grad, state, conj = exchange(k + 1, n_row, n_col, made[3], more)
            grads.append(grad)
            states.append(state)
    return tuple(last(n_row, n_col, tile, states[1:], targets, images, grads))


def solution(mesh):
    placed = (P(("row", "col"), None, None, None), P(("row", "col"), None), P(None, ("row", "col")))
    return jax.shard_map(
        body,
        mesh=mesh,
        in_specs=placed,
        out_specs=(P(None, ("row", "col")), P(None, ("row", "col"))),
        check_vma=False,
    )
```

```python
import functools

import jax
import jax.numpy as jnp
from jax import lax
from jax.experimental import pallas as pl
from jax.experimental.pallas import tpu as pltpu
from jax.sharding import PartitionSpec as P

MESH = pl.DeviceIdType.MESH
F32 = jnp.float32
BF16 = jnp.bfloat16
ITERS = 3
CBD = 8
N = 32
B = 128
MIB = 2**20


def dot(a, b, ca, cb, precision=None):
    return lax.dot_general(
        a, b, (((ca,), (cb,)), ((), ())), precision=precision, preferred_element_type=F32
    )


def exact(a, b, ca=1, cb=0):
    return dot(a, b, ca, cb, lax.Precision.HIGHEST)


def split(x):
    hi = x.astype(BF16)
    lo = (x - hi.astype(F32)).astype(BF16)
    return hi, lo


def stacked(x):
    hi, lo = split(x)
    return jnp.concatenate([hi, lo], axis=0)


def pack(square):
    return jnp.concatenate([square[8 * g : 8 * g + 8] for g in range(4)], axis=1)


def unpack(tile):
    return jnp.concatenate([tile[:, N * g : N * g + N] for g in range(4)], axis=0)


def fold(square):
    half = square[:N] + square[N:]
    return half[:, :N] + half[:, N:]


def spd_solve(matrix, right):
    table = jnp.concatenate([matrix, right], axis=1)
    wide = (8, 2 * N)
    parts = [table[8 * g : 8 * g + 8] for g in range(4)]
    sub = lax.broadcasted_iota(jnp.int32, wide, 0)

    def lanes(group, b):
        return jnp.broadcast_to(group[:, b : b + 1], wide)

    def rows(group, a):
        return jnp.broadcast_to(group[a : a + 1], wide)

    for g in range(4):
        mine = parts[g]
        pivots = [lanes(mine, 8 * g + b) for b in range(8)]
        factors = [[lanes(parts[h], 8 * g + b) for b in range(8)] if h != g else None for h in range(4)]
        for a in range(8):
            inverse = 1.0 / rows(pivots[a], a)
            here = sub == a
            factor = pivots[a]
            for b in range(a + 1, 8):
                scaled = rows(pivots[b], a) * inverse
                pivots[b] = jnp.where(here, scaled, pivots[b] - factor * scaled)
            scaled = rows(mine, a) * inverse
            mine = jnp.where(here, scaled, mine - factor * scaled)
        parts[g] = mine
        for h in range(4):
            if h != g:
                for b in range(8):
                    parts[h] = parts[h] - factors[h][b] * rows(mine, b)
    return jnp.concatenate(parts, axis=0)[:, N : 2 * N]


def apply_t(square, both):
    hi, lo = split(square.T)
    left = jnp.concatenate([jnp.concatenate([hi, hi], axis=1), jnp.concatenate([lo, lo], axis=1)], axis=0)
    out = dot(left, both, 1, 0)
    return out[:N] + out[N:]


COL, ORDER, FIRST, LAST, SOME = range(5)


def order_kernel(cols, table):
    count = cols.shape[1]
    shape = (count, count)
    row = cols[...].astype(F32)
    across = jnp.broadcast_to(row, shape)
    down = across.T
    p = lax.broadcasted_iota(jnp.int32, shape, 0).astype(F32)
    q = lax.broadcasted_iota(jnp.int32, shape, 1).astype(F32)
    one = jnp.ones(shape, F32)
    zero = jnp.zeros(shape, F32)
    before = jnp.where((across < down) | ((across == down) & (q < p)), one, zero)
    twins = jnp.where((across == down) & (q < p), one, zero)
    rank = jnp.sum(before, axis=1, keepdims=True)
    alone = jnp.where(jnp.sum(twins, axis=1, keepdims=True) == 0.0, 1.0, 0.0)
    place = rank == q
    table[COL : COL + 1, :] = cols[...]
    table[ORDER : ORDER + 1, :] = jnp.sum(jnp.where(place, p, zero), axis=0, keepdims=True).astype(jnp.int32)
    table[FIRST : FIRST + 1, :] = jnp.sum(jnp.where(place, alone, zero), axis=0, keepdims=True).astype(jnp.int32)
    upto = jnp.sum(jnp.where(down <= q, one, zero), axis=0, keepdims=True)
    table[LAST : LAST + 1, :] = jnp.maximum(upto - 1.0, 0.0).astype(jnp.int32)
    some = jnp.sum(jnp.where(down == q, one, zero), axis=0, keepdims=True)
    table[SOME : SOME + 1, :] = jnp.where(some > 0.0, 1.0, 0.0).astype(jnp.int32)
    table[5:8, :] = jnp.zeros((3, count), jnp.int32)


def order_of(cols):
    return pl.pallas_call(
        order_kernel, out_shape=jax.ShapeDtypeStruct((8, cols.shape[1]), jnp.int32)
    )(cols)


class Traffic:
    def __init__(self, send_sem, recv_sem):
        self.send_sem, self.recv_sem = send_sem, recv_sem
        self.sent = []

    def send(self, slot, src, dst, device):
        copy = pltpu.make_async_remote_copy(
            src_ref=src,
            dst_ref=dst,
            send_sem=self.send_sem.at[slot],
            recv_sem=self.recv_sem.at[slot],
            device_id=device,
            device_id_type=MESH,
        )
        copy.start()
        self.sent.append(copy)
        return copy

    def finish(self):
        for copy in self.sent:
            copy.wait_send()
        self.sent = []


class Plane:
    def __init__(self, row, col):
        z, x = row // 4, lax.rem(row, 4)

        def along_x(d):
            return (z * 4 + lax.rem(x + d, 4), col)

        def along_z(d):
            return (lax.rem(z + d, 4) * 4 + x, col)

        self.z, self.x = z, x
        self.halves = ((x, z, along_x, along_z), (z, x, along_z, along_x))


def chunk(ref, h, ta, tb, s):
    zz, xx = (tb, ta) if h == 0 else (ta, tb)
    return ref.at[zz, xx, h] if s is None else ref.at[zz, xx, h, pl.ds(2 * s, 2)]


RS_SLOTS = 60
AG_SLOTS = 40
SUM_SLOTS = 10
OFFSETS = (2, 3, 1, 0)


def reduce_scatter(sums, plane, r1, p1, r2, tr, hook):
    c1, c2 = {}, {}
    halves = plane.halves

    def send1(u, h, idx):
        pa, pb, ring, _ = halves[h]
        tb = lax.rem(pb + OFFSETS[u], 4)
        off, s, d = ((2, 0, 1), (2, 1, 3), (1, 1, 1), (3, 0, 3))[idx]
        src = chunk(sums, h, lax.rem(pa + off, 4), tb, s)
        c1[u, h, idx] = tr.send((h * 4 + u) * 6 + idx, src, r1.at[h, u, idx], ring(d))

    def pass_on(u, h):
        pa, pb, ring, _ = halves[h]
        tb = lax.rem(pb + OFFSETS[u], 4)
        for idx, off, d in ((0, 1, 1), (1, 3, 3)):
            c1[u, h, idx].wait_recv()
            r1[h, u, idx] += chunk(sums, h, lax.rem(pa + off, 4), tb, idx)[...]
            c1[u, h, 4 + idx] = tr.send(
                (h * 4 + u) * 6 + 4 + idx, r1.at[h, u, idx], r1.at[h, u, 4 + idx], ring(d)
            )

    def send2(h, idx, src, d):
        c2[h, idx] = tr.send(48 + h * 6 + idx, src, r2.at[h, idx], halves[h][3](d))

    def close(u, h):
        pa, pb, _, _ = halves[h]
        tb = lax.rem(pb + OFFSETS[u], 4)
        for idx in (2, 3, 4, 5):
            c1[u, h, idx].wait_recv()
        p1[h, u, 0:2] = chunk(sums, h, pa, tb, 0)[...] + (r1[h, u, 3] + r1[h, u, 4])
        p1[h, u, 2:4] = chunk(sums, h, pa, tb, 1)[...] + (r1[h, u, 2] + r1[h, u, 5])
        if u == 0:
            send2(h, 0, p1.at[h, 0, pl.ds(0, 2)], 1)
            send2(h, 1, p1.at[h, 0, pl.ds(2, 2)], 3)
        if u == 1:
            send2(h, 3, p1.at[h, 1, pl.ds(0, 2)], 3)
            c2[h, 1].wait_recv()
            r2[h, 1] += p1[h, 1, 2:4]
            send2(h, 5, r2.at[h, 1], 3)
        if u == 2:
            send2(h, 2, p1.at[h, 2, pl.ds(2, 2)], 1)
            c2[h, 0].wait_recv()
            r2[h, 0] += p1[h, 2, 0:2]
            send2(h, 4, r2.at[h, 0], 1)

    both = range(2)
    for u in range(4):
        for h in both:
            send1(u, h, 0)
            send1(u, h, 1)
    for h in both:
        send1(0, h, 2)
        send1(0, h, 3)
    hook(-1)
    for u in range(5):
        if u < 4:
            for h in both:
                pass_on(u, h)
            if u < 3:
                for h in both:
                    send1(u + 1, h, 2)
                    send1(u + 1, h, 3)
        if u >= 1:
            for h in both:
                close(u - 1, h)
        hook(u)
    own = []
    for h in both:
        for idx in (2, 3, 4, 5):
            c2[h, idx].wait_recv()
        first = p1[h, 3, 0:2] + (r2[h, 3] + r2[h, 4])
        second = p1[h, 3, 2:4] + (r2[h, 2] + r2[h, 5])
        own += [first[0], first[1], second[0], second[1]]
    tr.finish()
    return jnp.concatenate(own, axis=1)


HOPS = ((0, None, 1), (0, None, 3), (3, 0, 1), (1, 1, 3))


def gather_all(vec, plane, tr, hook):
    halves = plane.halves
    order = (0, 3, 1, 2)
    c1, c2 = {}, {}

    def send1(h, idx):
        pa, pb, _, ring = halves[h]
        off, s, d = HOPS[idx]
        ref = chunk(vec, h, pa, lax.rem(pb + off, 4), s)
        c1[h, idx] = tr.send(RS_SLOTS + h * 4 + idx, ref, ref, ring(d))

    def send2(h, v, idx):
        pa, pb, ring, _ = halves[h]
        tb = lax.rem(pb + order[v], 4)
        off, s, d = HOPS[idx]
        ref = chunk(vec, h, lax.rem(pa + off, 4), tb, s)
        c2[h, v, idx] = tr.send(RS_SLOTS + 8 + (h * 4 + v) * 4 + idx, ref, ref, ring(d))

    both = range(2)

    def unit(v):
        for h in both:
            send2(h, v, 0)
            send2(h, v, 1)

    def pass_on(v):
        for h in both:
            for idx in range(2):
                c2[h, v, idx].wait_recv()
                send2(h, v, 2 + idx)

    for h in both:
        send1(h, 0)
        send1(h, 1)
    unit(0)
    hook(0)
    for h in both:
        for idx in range(2):
            c1[h, idx].wait_recv()
            send1(h, 2 + idx)
    unit(1)
    pass_on(0)
    unit(2)
    hook(1)
    for h in both:
        c1[h, 2].wait_recv()
        c1[h, 3].wait_recv()
    unit(3)
    pass_on(1)
    hook(2)
    pass_on(2)
    hook(3)
    pass_on(3)
    hook(4)
    for v in range(4):
        for h in both:
            c2[h, v, 2].wait_recv()
            c2[h, v, 3].wait_recv()
    tr.finish()


def sum_stages(row, col, n_col):
    n_y = n_col // 2
    z, x = row // 4, lax.rem(row, 4)
    y, core = col // 2, lax.rem(col, 2)
    return [
        ([(row, y * 2 + 1 - core)], core, 2),
        ([(row, lax.rem(y + d, n_y) * 2 + core) for d in range(1, n_y)], y, n_y),
        ([(z * 4 + lax.rem(x + d, 4), col) for d in range(1, 4)], x, 4),
        ([(lax.rem(z + d, 4) * 4 + x, col) for d in range(1, 4)], z, 4),
    ]


class TileSum:
    def __init__(self, stages, tr, slot, box, rows):
        self.stages, self.tr, self.slot, self.box, self.rows = stages, tr, slot, box, rows
        self.at, self.open = 0, []

    def put(self, tile):
        peers, me, _ = self.stages[self.at]
        ref = self.box.at[self.at, me, pl.ds(0, self.rows)]
        self.box[self.at, me, 0 : self.rows] = tile
        self.open = []
        for device in peers:
            self.open.append(self.tr.send(self.slot, ref, ref, device))
            self.slot += 1

    def take(self):
        for c in self.open:
            c.wait_recv()
        total = self.box[self.at, 0, 0 : self.rows]
        for i in range(1, self.stages[self.at][2]):
            total = total + self.box[self.at, i, 0 : self.rows]
        self.at += 1
        return total

    def step(self):
        self.put(self.take())


GG, IG, MIX, STEP = range(4)
ROWS = 64
UNROLL = 8
LOAD = 4
SLOTS = 4


def rows_loop(lo, hi, width, step):
    def some(o, carry):
        for j in range(width):
            step(lo + o * width + j)
        return carry

    lax.fori_loop(0, (hi - lo) // width, some, 0)


def cgls_kernel(n_col, table, blocks, targets, sol, res, *scratch):
    across, down, pieces, running, sums, vec, parts, images, t_mem, grads = scratch[:10]
    conj, gram_acc, small, r1, p1, r2, box, send_sem, recv_sem, load_sem = scratch[10:]
    row, col = lax.axis_index("row"), lax.axis_index("col")
    plane = Plane(row, col)
    stages = sum_stages(row, col, n_col)
    tr, tr_small = Traffic(send_sem, recv_sem), Traffic(send_sem, recv_sem)

    size = LOAD * 16

    def load(step):
        slot = lax.rem(step, SLOTS)
        return pltpu.make_async_copy(
            blocks.at[pl.ds(step * size, size)], running.at[pl.ds(slot * size, size)], load_sem.at[slot]
        )

    read_targets = pltpu.make_async_copy(targets, t_mem, load_sem.at[SLOTS])
    read_targets.start()
    for s in range(SLOTS):
        load(s).start()

    barrier = pltpu.get_barrier_semaphore()
    who = [device for peers, _, _ in stages for device in peers]
    for device in who:
        pl.semaphore_signal(barrier, inc=1, device_id=device, device_id_type=MESH)

    def lanes(i):
        return pl.ds(pl.multiple_of(i * B, B), B)

    def piece(i, both, block):
        out = dot(jnp.concatenate([both, both], axis=1), block, 1, 0)
        out = out[:N] + out[N:]
        for k in range(4):
            pieces[i * 4 + k] = out[:, k * B : (k + 1) * B]

    read_targets.wait()

    def first(step, carry):
        load(step).wait()
        slot = lax.rem(step, SLOTS)
        for j in range(LOAD):
            i = step * LOAD + j
            his, los = [], []
            for k in range(4):
                base = slot * size + j * 16 + k * 4
                hi, lo = split(jnp.concatenate([running[base + q] for q in range(4)], axis=0))
                his.append(hi)
                los.append(lo)
            block = jnp.concatenate([jnp.concatenate(his, axis=1), jnp.concatenate(los, axis=1)], axis=0)
            across[i] = block
            piece(i, stacked(t_mem[:, lanes(i)]), block)

        @pl.when(step + SLOTS < ROWS // LOAD)
        def _():
            load(step + SLOTS).start()

        return carry

    lax.fori_loop(0, ROWS // LOAD, first, 0)

    def add_up():
        def run(o, total):
            for j in range(8):
                p = o * 8 + j
                total = jnp.where(table[FIRST, p] == 1, 0.0, total) + pieces[table[ORDER, p]]
                running[p] = total
            return total

        lax.fori_loop(0, ROWS * 4 // 8, run, jnp.zeros((N, B), F32))

        def pick(owner, carry):
            for h in range(2):
                for j in range(4):
                    c = owner * CBD + 4 * h + j
                    value = jnp.where(table[SOME, c] == 1, running[table[LAST, c]], 0.0)
                    sums[owner // 4, lax.rem(owner, 4), h, j] = value
            return carry

        lax.fori_loop(0, 16, pick, 0)

    def turn(i):
        for k in range(4):
            for h in range(2):
                tile = across[i, h * B : (h + 1) * B, k * B : (k + 1) * B]
                down[i, k * B : (k + 1) * B, h * B : (h + 1) * B] = tile.T

    def forward(at):
        def one(i):
            picked = jnp.concatenate([parts[table[COL, i * 4 + j]] for j in range(4)], axis=1)
            quad = dot(picked, down[i], 1, 0)
            quad = quad[:N] + quad[N:]
            images[at : at + 2 * N, lanes(i)] = stacked(quad[:, :B] + quad[:, B:])

        return one

    def backward(at):
        def one(i):
            piece(i, images[at : at + 2 * N, lanes(i)], across[i])

        return one

    def image_grams(k):
        gram_acc[...] = jnp.zeros_like(gram_acc)
        width = 1024

        def strip(s, carry):
            at = pl.ds(pl.multiple_of(s * width, width), width)
            mine = images[2 * N * k : 2 * N * (k + 1), at]
            gram_acc[:, 0 : 2 * N * (k + 1)] += dot(mine, images[0 : 2 * N * (k + 1), at], 1, 1)
            return carry

        lax.fori_loop(0, ROWS * B // width, strip, 0)
        return jnp.concatenate(
            [pack(fold(gram_acc[:, 2 * N * j : 2 * N * (j + 1)])) for j in range(k, -1, -1)], axis=0
        )

    def mix_of(k):
        if k:
            small[k, MIX] = spd_solve(small[k - 1, GG], small[k, GG])

    def image_gram_of(k, total):
        gram = unpack(total[0:8])
        if k:
            mix = small[k, MIX]
            cross = unpack(total[8:16])
            if k == 2:
                cross = cross + exact(unpack(total[16:24]), small[1, MIX])
            mixed = exact(cross, mix)
            gram = gram + (mixed + mixed.T) + exact(mix, exact(small[k - 1, IG], mix), 0, 0)
        small[k, IG] = gram

    def cut(owner, carry):
        for h in range(2):
            for j in range(4):
                parts[owner * CBD + 4 * h + j] = stacked(vec[owner // 4, lax.rem(owner, 4), h, j])
        return carry

    add_up()
    pl.semaphore_wait(barrier, len(who))
    slot0 = RS_SLOTS + AG_SLOTS
    turned = {-1: (0, 12), 0: (12, 16), 1: (16, 20), 2: (20, 24), 3: (24, 28), 4: (28, 32)}
    turned_later = {0: (32, 42), 1: (42, 50), 2: (50, 56), 3: (56, 60), 4: (60, 64)}
    image_total = None
    for k in range(ITERS):

        def beside_first(u, k=k):
            if k == 0:
                rows_loop(*turned[u], 2, turn)
            elif u == -1:
                mix_of(k - 1)
            elif u == 0:
                image_gram_of(k - 1, image_total)
            elif u == 1:
                small[k - 1, STEP] = spd_solve(small[k - 1, IG], small[k - 1, GG])

        fresh = reduce_scatter(sums, plane, r1, p1, r2, tr, beside_first)
        if k == 0:
            grad = fresh
        else:
            direction = fresh if k == 1 else fresh + apply_t(small[1, MIX], stacked(conj[...]))
            grad = grads[k - 1] - apply_t(small[k - 1, STEP], stacked(direction))
        for h in range(2):
            for j in range(4):
                at = (4 * h + j) * B
                vec[plane.z, plane.x, h, j] = grad[:, at : at + B]
        grad_sum = TileSum(stages, tr_small, slot0 + 2 * k * SUM_SLOTS, box.at[2 * k], 8)

        def beside_second(v, k=k):
            if v == 0:
                both = stacked(grad)
                grad_sum.put(pack(fold(dot(both, both, 1, 1))))
                grads[k] = grad
                if k:
                    conj[...] = direction
            if v == 2:
                grad_sum.step()
            if k == 0:
                rows_loop(*turned_later[v], 2, turn)

        gather_all(vec, plane, tr, beside_second)
        grad_sum.step()
        lax.fori_loop(0, 16, cut, 0)
        rows_loop(0, ROWS // 2, UNROLL, forward(2 * N * k))
        grad_sum.step()
        rows_loop(ROWS // 2, ROWS, UNROLL, forward(2 * N * k))
        small[k, GG] = unpack(grad_sum.take())
        image_sum = TileSum(stages, tr_small, slot0 + (2 * k + 1) * SUM_SLOTS, box.at[2 * k + 1], 8 * (k + 1))
        image_sum.put(image_grams(k))
        if k + 1 < ITERS:
            rows_loop(0, 24, UNROLL, backward(2 * N * k))
            image_sum.step()
            rows_loop(24, 40, UNROLL, backward(2 * N * k))
            image_sum.step()
            rows_loop(40, ROWS, UNROLL, backward(2 * N * k))
            image_sum.step()
            add_up()
            image_total = image_sum.take()
        else:
            mix_of(k)
            for _ in range(3):
                image_sum.step()
            image_gram_of(k, image_sum.take())

    e2 = spd_solve(small[2, IG], small[2, GG])
    e1 = small[1, STEP] + exact(small[2, MIX], e2)
    e0 = small[0, STEP] + exact(small[1, MIX], e1)
    his, los = [], []
    for e in (e0, e1, e2):
        hi, lo = split(e.T)
        his += [hi, hi]
        los += [lo, lo]
    left = jnp.concatenate([jnp.concatenate(his, axis=1), jnp.concatenate(los, axis=1)], axis=0)
    out = dot(left, jnp.concatenate([stacked(grads[j]) for j in range(3)], axis=0), 1, 0)
    sol[...] = out[:N] + out[N:]
    width = 1024

    def strip(s, carry):
        at = pl.ds(pl.multiple_of(s * width, width), width)
        out = dot(left, images[:, at], 1, 0)
        res[:, at] = t_mem[:, at] - (out[:N] + out[N:])
        return carry

    lax.fori_loop(0, ROWS * B // width, strip, 0)
    tr_small.finish()


def body(blocks, block_cols, targets):
    n_row = lax.axis_size("row")
    n_col = lax.axis_size("col")
    group = CBD * n_row
    flat = block_cols.reshape(1, -1)
    table = order_of(flat // (CBD * n_col) * CBD + lax.rem(flat, CBD))
    vmem = pl.BlockSpec(memory_space=pltpu.VMEM)
    anywhere = pl.BlockSpec(memory_space=pl.ANY)
    width = CBD * B
    chunks = (4, 4, 2, CBD // 2, N, B)
    slots = RS_SLOTS + AG_SLOTS + 6 * SUM_SLOTS
    return tuple(
        pl.pallas_call(
            functools.partial(cgls_kernel, n_col),
            out_shape=[jax.ShapeDtypeStruct((N, width), F32), jax.ShapeDtypeStruct(targets.shape, F32)],
            in_specs=[pl.BlockSpec(memory_space=pltpu.SMEM), anywhere, anywhere],
            out_specs=[vmem] * 2,
            scratch_shapes=[
                pltpu.VMEM((ROWS, 2 * B, 4 * B), BF16),
                pltpu.VMEM((ROWS, 4 * B, 2 * B), BF16),
                pltpu.VMEM((ROWS * 4, N, B), F32),
                pltpu.VMEM((ROWS * 4, N, B), F32),
                pltpu.VMEM(chunks, F32),
                pltpu.VMEM(chunks, F32),
                pltpu.VMEM((group, 2 * N, B), BF16),
                pltpu.VMEM((2 * N * ITERS, ROWS * B), BF16),
                pltpu.VMEM((N, ROWS * B), F32),
                pltpu.VMEM((ITERS, N, width), F32),
                pltpu.VMEM((N, width), F32),
                pltpu.VMEM((2 * N, 2 * N * 4), F32),
                pltpu.VMEM((ITERS, 4, N, N), F32),
                pltpu.VMEM((2, 4, 6, 2, N, B), F32),
                pltpu.VMEM((2, 4, 4, N, B), F32),
                pltpu.VMEM((2, 6, 2, N, B), F32),
                pltpu.VMEM((6, 4, 4, 24, B), F32),
                pltpu.SemaphoreType.DMA((slots,)),
                pltpu.SemaphoreType.DMA((slots,)),
                pltpu.SemaphoreType.DMA((SLOTS + 1,)),
            ],
            compiler_params=pltpu.CompilerParams(
                collective_id=0, has_side_effects=True, vmem_limit_bytes=60 * MIB
            ),
        )(table, blocks.reshape(-1, N, B), targets)
    )


def solution(mesh):
    placed = (P(("row", "col"), None, None, None), P(("row", "col"), None), P(None, ("row", "col")))
    return jax.shard_map(
        body,
        mesh=mesh,
        in_specs=placed,
        out_specs=(P(None, ("row", "col")), P(None, ("row", "col"))),
        check_vma=False,
    )
```

```python
import functools

import jax
import jax.numpy as jnp
from jax import lax
from jax.experimental import pallas as pl
from jax.experimental.pallas import tpu as pltpu
from jax.sharding import PartitionSpec as P

MESH = pl.DeviceIdType.MESH
F32 = jnp.float32
BF16 = jnp.bfloat16
ITERS = 3
CBD = 8
N = 32
B = 128
MIB = 2**20


def dot(a, b, ca, cb, precision=None):
    return lax.dot_general(
        a, b, (((ca,), (cb,)), ((), ())), precision=precision, preferred_element_type=F32
    )


def exact(a, b, ca=1, cb=0):
    return dot(a, b, ca, cb, lax.Precision.HIGHEST)


def split(x):
    hi = x.astype(BF16)
    lo = (x - hi.astype(F32)).astype(BF16)
    return hi, lo


def stacked(x):
    hi, lo = split(x)
    return jnp.concatenate([hi, lo], axis=0)


def pack(square):
    return jnp.concatenate([square[8 * g : 8 * g + 8] for g in range(4)], axis=1)


def unpack(tile):
    return jnp.concatenate([tile[:, N * g : N * g + N] for g in range(4)], axis=0)


def fold(square):
    half = square[:N] + square[N:]
    return half[:, :N] + half[:, N:]


def spd_solve(matrix, right):
    table = jnp.concatenate([matrix, right], axis=1)
    wide = (8, 2 * N)
    parts = [table[8 * g : 8 * g + 8] for g in range(4)]
    sub = lax.broadcasted_iota(jnp.int32, wide, 0)

    def lanes(group, b):
        return jnp.broadcast_to(group[:, b : b + 1], wide)

    def rows(group, a):
        return jnp.broadcast_to(group[a : a + 1], wide)

    for g in range(4):
        mine = parts[g]
        pivots = [lanes(mine, 8 * g + b) for b in range(8)]
        factors = [[lanes(parts[h], 8 * g + b) for b in range(8)] if h != g else None for h in range(4)]
        for a in range(8):
            inverse = 1.0 / rows(pivots[a], a)
            here = sub == a
            factor = pivots[a]
            for b in range(a + 1, 8):
                scaled = rows(pivots[b], a) * inverse
                pivots[b] = jnp.where(here, scaled, pivots[b] - factor * scaled)
            scaled = rows(mine, a) * inverse
            mine = jnp.where(here, scaled, mine - factor * scaled)
        parts[g] = mine
        for h in range(4):
            if h != g:
                for b in range(8):
                    parts[h] = parts[h] - factors[h][b] * rows(mine, b)
    return jnp.concatenate(parts, axis=0)[:, N : 2 * N]


def apply_t(square, both):
    hi, lo = split(square.T)
    left = jnp.concatenate([jnp.concatenate([hi, hi], axis=1), jnp.concatenate([lo, lo], axis=1)], axis=0)
    out = dot(left, both, 1, 0)
    return out[:N] + out[N:]


COL, ORDER, FIRST, LAST, SOME = range(5)


def order_kernel(cols, table):
    count = cols.shape[1]
    shape = (count, count)
    row = cols[...].astype(F32)
    across = jnp.broadcast_to(row, shape)
    down = across.T
    p = lax.broadcasted_iota(jnp.int32, shape, 0).astype(F32)
    q = lax.broadcasted_iota(jnp.int32, shape, 1).astype(F32)
    one = jnp.ones(shape, F32)
    zero = jnp.zeros(shape, F32)
    before = jnp.where((across < down) | ((across == down) & (q < p)), one, zero)
    twins = jnp.where((across == down) & (q < p), one, zero)
    rank = jnp.sum(before, axis=1, keepdims=True)
    alone = jnp.where(jnp.sum(twins, axis=1, keepdims=True) == 0.0, 1.0, 0.0)
    place = rank == q
    table[COL : COL + 1, :] = cols[...]
    table[ORDER : ORDER + 1, :] = jnp.sum(jnp.where(place, p, zero), axis=0, keepdims=True).astype(jnp.int32)
    table[FIRST : FIRST + 1, :] = jnp.sum(jnp.where(place, alone, zero), axis=0, keepdims=True).astype(jnp.int32)
    upto = jnp.sum(jnp.where(down <= q, one, zero), axis=0, keepdims=True)
    table[LAST : LAST + 1, :] = jnp.maximum(upto - 1.0, 0.0).astype(jnp.int32)
    some = jnp.sum(jnp.where(down == q, one, zero), axis=0, keepdims=True)
    table[SOME : SOME + 1, :] = jnp.where(some > 0.0, 1.0, 0.0).astype(jnp.int32)
    table[5:8, :] = jnp.zeros((3, count), jnp.int32)


def order_of(cols):
    return pl.pallas_call(
        order_kernel, out_shape=jax.ShapeDtypeStruct((8, cols.shape[1]), jnp.int32)
    )(cols)


class Traffic:
    def __init__(self, send_sem, recv_sem):
        self.send_sem, self.recv_sem = send_sem, recv_sem
        self.sent = []

    def send(self, slot, src, dst, device):
        copy = pltpu.make_async_remote_copy(
            src_ref=src,
            dst_ref=dst,
            send_sem=self.send_sem.at[slot],
            recv_sem=self.recv_sem.at[slot],
            device_id=device,
            device_id_type=MESH,
        )
        copy.start()
        self.sent.append(copy)
        return copy

    def finish(self):
        for copy in self.sent:
            copy.wait_send()
        self.sent = []


class Plane:
    def __init__(self, row, col):
        z, x = row // 4, lax.rem(row, 4)

        def along_x(d):
            return (z * 4 + lax.rem(x + d, 4), col)

        def along_z(d):
            return (lax.rem(z + d, 4) * 4 + x, col)

        self.z, self.x = z, x
        self.halves = ((x, z, along_x, along_z), (z, x, along_z, along_x))


def chunk(ref, h, ta, tb, s):
    zz, xx = (tb, ta) if h == 0 else (ta, tb)
    return ref.at[zz, xx, h] if s is None else ref.at[zz, xx, h, pl.ds(2 * s, 2)]


RS_SLOTS = 60
AG_SLOTS = 40
SUM_SLOTS = 22
OFFSETS = (2, 3, 1, 0)


def reduce_scatter(sums, plane, r1, p1, r2, tr, hook):
    c1, c2 = {}, {}
    halves = plane.halves

    def send1(u, h, idx):
        pa, pb, ring, _ = halves[h]
        tb = lax.rem(pb + OFFSETS[u], 4)
        off, s, d = ((2, 0, 1), (2, 1, 3), (1, 1, 1), (3, 0, 3))[idx]
        src = chunk(sums, h, lax.rem(pa + off, 4), tb, s)
        c1[u, h, idx] = tr.send((h * 4 + u) * 6 + idx, src, r1.at[h, u, idx], ring(d))

    def pass_on(u, h):
        pa, pb, ring, _ = halves[h]
        tb = lax.rem(pb + OFFSETS[u], 4)
        for idx, off, d in ((0, 1, 1), (1, 3, 3)):
            c1[u, h, idx].wait_recv()
            r1[h, u, idx] += chunk(sums, h, lax.rem(pa + off, 4), tb, idx)[...]
            c1[u, h, 4 + idx] = tr.send(
                (h * 4 + u) * 6 + 4 + idx, r1.at[h, u, idx], r1.at[h, u, 4 + idx], ring(d)
            )

    def send2(h, idx, src, d):
        c2[h, idx] = tr.send(48 + h * 6 + idx, src, r2.at[h, idx], halves[h][3](d))

    def close(u, h):
        pa, pb, _, _ = halves[h]
        tb = lax.rem(pb + OFFSETS[u], 4)
        for idx in (2, 3, 4, 5):
            c1[u, h, idx].wait_recv()
        p1[h, u, 0:2] = chunk(sums, h, pa, tb, 0)[...] + (r1[h, u, 3] + r1[h, u, 4])
        p1[h, u, 2:4] = chunk(sums, h, pa, tb, 1)[...] + (r1[h, u, 2] + r1[h, u, 5])
        if u == 0:
            send2(h, 0, p1.at[h, 0, pl.ds(0, 2)], 1)
            send2(h, 1, p1.at[h, 0, pl.ds(2, 2)], 3)
        if u == 1:
            send2(h, 3, p1.at[h, 1, pl.ds(0, 2)], 3)
            c2[h, 1].wait_recv()
            r2[h, 1] += p1[h, 1, 2:4]
            send2(h, 5, r2.at[h, 1], 3)
        if u == 2:
            send2(h, 2, p1.at[h, 2, pl.ds(2, 2)], 1)
            c2[h, 0].wait_recv()
            r2[h, 0] += p1[h, 2, 0:2]
            send2(h, 4, r2.at[h, 0], 1)

    both = range(2)
    for u in range(4):
        for h in both:
            send1(u, h, 0)
            send1(u, h, 1)
    for h in both:
        send1(0, h, 2)
        send1(0, h, 3)
    hook(-1)
    for u in range(5):
        if u < 4:
            for h in both:
                pass_on(u, h)
            if u < 3:
                for h in both:
                    send1(u + 1, h, 2)
                    send1(u + 1, h, 3)
        if u >= 1:
            for h in both:
                close(u - 1, h)
        hook(u)
    own = []
    for h in both:
        for idx in (2, 3, 4, 5):
            c2[h, idx].wait_recv()
        first = p1[h, 3, 0:2] + (r2[h, 3] + r2[h, 4])
        second = p1[h, 3, 2:4] + (r2[h, 2] + r2[h, 5])
        own += [first[0], first[1], second[0], second[1]]
    tr.finish()
    return jnp.concatenate(own, axis=1)


HOPS = ((0, None, 1), (0, None, 3), (3, 0, 1), (1, 1, 3))


def gather_all(vec, plane, tr, hook):
    halves = plane.halves
    order = (0, 3, 1, 2)
    c1, c2 = {}, {}

    def send1(h, idx):
        pa, pb, _, ring = halves[h]
        off, s, d = HOPS[idx]
        ref = chunk(vec, h, pa, lax.rem(pb + off, 4), s)
        c1[h, idx] = tr.send(RS_SLOTS + h * 4 + idx, ref, ref, ring(d))

    def send2(h, v, idx):
        pa, pb, ring, _ = halves[h]
        tb = lax.rem(pb + order[v], 4)
        off, s, d = HOPS[idx]
        ref = chunk(vec, h, lax.rem(pa + off, 4), tb, s)
        c2[h, v, idx] = tr.send(RS_SLOTS + 8 + (h * 4 + v) * 4 + idx, ref, ref, ring(d))

    both = range(2)

    def unit(v):
        for h in both:
            send2(h, v, 0)
            send2(h, v, 1)

    def pass_on(v):
        for h in both:
            for idx in range(2):
                c2[h, v, idx].wait_recv()
                send2(h, v, 2 + idx)

    for h in both:
        send1(h, 0)
        send1(h, 1)
    unit(0)
    hook(0)
    for h in both:
        for idx in range(2):
            c1[h, idx].wait_recv()
            send1(h, 2 + idx)
    unit(1)
    pass_on(0)
    unit(2)
    hook(1)
    for h in both:
        c1[h, 2].wait_recv()
        c1[h, 3].wait_recv()
    unit(3)
    pass_on(1)
    hook(2)
    pass_on(2)
    hook(3)
    pass_on(3)
    hook(4)
    for v in range(4):
        for h in both:
            c2[h, v, 2].wait_recv()
            c2[h, v, 3].wait_recv()
    tr.finish()


def sum_stages(row, col, n_row, n_col):
    z, x = row // 4, lax.rem(row, 4)
    along_x = ([(z * 4 + lax.rem(x + d, 4), col) for d in range(1, 4)], x, 4)
    along_z = ([(lax.rem(z + d, 4) * 4 + x, col) for d in range(1, 4)], z, 4)
    plane = ([(lax.rem(row + d, n_row), col) for d in range(1, n_row)], row, n_row)
    across = ([(row, lax.rem(col + d, n_col)) for d in range(1, n_col)], col, n_col)
    return along_x, along_z, plane, across


class TileSum:
    def __init__(self, stages, tr, slot, box, rows):
        self.stages, self.tr, self.slot, self.box, self.rows = stages, tr, slot, box, rows
        self.at, self.open = 0, []

    def put(self, tile):
        peers, me, _ = self.stages[self.at]
        ref = self.box.at[self.at, me, pl.ds(0, self.rows)]
        self.box[self.at, me, 0 : self.rows] = tile
        self.open = []
        for device in peers:
            self.open.append(self.tr.send(self.slot, ref, ref, device))
            self.slot += 1

    def take(self):
        for c in self.open:
            c.wait_recv()
        total = self.box[self.at, 0, 0 : self.rows]
        for i in range(1, self.stages[self.at][2]):
            total = total + self.box[self.at, i, 0 : self.rows]
        self.at += 1
        return total

    def step(self):
        self.put(self.take())


GG, IG, MIX, STEP = range(4)
ROWS = 64
UNROLL = 8
LOAD = 4
SLOTS = 4


def rows_loop(lo, hi, width, step):
    def some(o, carry):
        for j in range(width):
            step(lo + o * width + j)
        return carry

    lax.fori_loop(0, (hi - lo) // width, some, 0)


def cgls_kernel(n_row, n_col, table, blocks, targets, sol, res, *scratch):
    across, down, pieces, running, sums, vec, parts, images, t_mem, grads = scratch[:10]
    conj, gram_acc, small, r1, p1, r2, box, send_sem, recv_sem, load_sem = scratch[10:]
    row, col = lax.axis_index("row"), lax.axis_index("col")
    plane = Plane(row, col)
    along_x, along_z, in_plane, across_it = sum_stages(row, col, n_row, n_col)
    tr, tr_small = Traffic(send_sem, recv_sem), Traffic(send_sem, recv_sem)

    size = LOAD * 16

    def load(step):
        slot = lax.rem(step, SLOTS)
        return pltpu.make_async_copy(
            blocks.at[pl.ds(step * size, size)], running.at[pl.ds(slot * size, size)], load_sem.at[slot]
        )

    read_targets = pltpu.make_async_copy(targets, t_mem, load_sem.at[SLOTS])
    read_targets.start()
    for s in range(SLOTS):
        load(s).start()

    barrier = pltpu.get_barrier_semaphore()
    who = in_plane[0] + across_it[0]
    for device in who:
        pl.semaphore_signal(barrier, inc=1, device_id=device, device_id_type=MESH)

    def lanes(i):
        return pl.ds(pl.multiple_of(i * B, B), B)

    def piece(i, both, block):
        out = dot(jnp.concatenate([both, both], axis=1), block, 1, 0)
        out = out[:N] + out[N:]
        for k in range(4):
            pieces[i * 4 + k] = out[:, k * B : (k + 1) * B]

    read_targets.wait()

    def first(step, carry):
        load(step).wait()
        slot = lax.rem(step, SLOTS)
        for j in range(LOAD):
            i = step * LOAD + j
            his, los = [], []
            for k in range(4):
                base = slot * size + j * 16 + k * 4
                hi, lo = split(jnp.concatenate([running[base + q] for q in range(4)], axis=0))
                his.append(hi)
                los.append(lo)
            block = jnp.concatenate([jnp.concatenate(his, axis=1), jnp.concatenate(los, axis=1)], axis=0)
            across[i] = block
            piece(i, stacked(t_mem[:, lanes(i)]), block)

        @pl.when(step + SLOTS < ROWS // LOAD)
        def _():
            load(step + SLOTS).start()

        return carry

    lax.fori_loop(0, ROWS // LOAD, first, 0)

    def add_up():
        def run(o, total):
            for j in range(8):
                p = o * 8 + j
                total = jnp.where(table[FIRST, p] == 1, 0.0, total) + pieces[table[ORDER, p]]
                running[p] = total
            return total

        lax.fori_loop(0, ROWS * 4 // 8, run, jnp.zeros((N, B), F32))

        def pick(owner, carry):
            for h in range(2):
                for j in range(4):
                    c = owner * CBD + 4 * h + j
                    value = jnp.where(table[SOME, c] == 1, running[table[LAST, c]], 0.0)
                    sums[owner // 4, lax.rem(owner, 4), h, j] = value
            return carry

        lax.fori_loop(0, 16, pick, 0)

    def turn(i):
        for k in range(4):
            for h in range(2):
                tile = across[i, h * B : (h + 1) * B, k * B : (k + 1) * B]
                down[i, k * B : (k + 1) * B, h * B : (h + 1) * B] = tile.T

    def forward(at):
        def one(i):
            picked = jnp.concatenate([parts[table[COL, i * 4 + j]] for j in range(4)], axis=1)
            quad = dot(picked, down[i], 1, 0)
            quad = quad[:N] + quad[N:]
            images[at : at + 2 * N, lanes(i)] = stacked(quad[:, :B] + quad[:, B:])

        return one

    def backward(at):
        def one(i):
            piece(i, images[at : at + 2 * N, lanes(i)], across[i])

        return one

    def image_grams(k):
        gram_acc[...] = jnp.zeros_like(gram_acc)
        width = 1024

        def strip(s, carry):
            at = pl.ds(pl.multiple_of(s * width, width), width)
            mine = images[2 * N * k : 2 * N * (k + 1), at]
            gram_acc[:, 0 : 2 * N * (k + 1)] += dot(mine, images[0 : 2 * N * (k + 1), at], 1, 1)
            return carry

        lax.fori_loop(0, ROWS * B // width, strip, 0)
        return jnp.concatenate(
            [pack(fold(gram_acc[:, 2 * N * j : 2 * N * (j + 1)])) for j in range(k, -1, -1)], axis=0
        )

    def mix_of(k):
        if k:
            small[k, MIX] = spd_solve(small[k - 1, GG], small[k, GG])

    def image_gram_of(k, total):
        gram = unpack(total[0:8])
        if k:
            mix = small[k, MIX]
            cross = unpack(total[8:16])
            if k == 2:
                cross = cross + exact(unpack(total[16:24]), small[1, MIX])
            mixed = exact(cross, mix)
            gram = gram + (mixed + mixed.T) + exact(mix, exact(small[k - 1, IG], mix), 0, 0)
        small[k, IG] = gram

    def cut(owner, carry):
        for h in range(2):
            for j in range(4):
                parts[owner * CBD + 4 * h + j] = stacked(vec[owner // 4, lax.rem(owner, 4), h, j])
        return carry

    add_up()
    pl.semaphore_wait(barrier, len(who))
    slot0 = RS_SLOTS + AG_SLOTS
    turned = {-1: (0, 12), 0: (12, 16), 1: (16, 20), 2: (20, 24), 3: (24, 28), 4: (28, 32)}
    turned_later = {0: (32, 42), 1: (42, 50), 2: (50, 56), 3: (56, 60), 4: (60, 64)}
    image_sum = None
    for k in range(ITERS):

        def beside_first(u, k=k):
            if k == 0:
                rows_loop(*turned[u], 2, turn)
            elif u == -1:
                mix_of(k - 1)
            elif u == 0:
                image_gram_of(k - 1, image_sum.take())
            elif u == 1:
                small[k - 1, STEP] = spd_solve(small[k - 1, IG], small[k - 1, GG])

        fresh = reduce_scatter(sums, plane, r1, p1, r2, tr, beside_first)
        if k == 0:
            grad = fresh
        else:
            direction = fresh if k == 1 else fresh + apply_t(small[1, MIX], stacked(conj[...]))
            grad = grads[k - 1] - apply_t(small[k - 1, STEP], stacked(direction))
        for h in range(2):
            for j in range(4):
                at = (4 * h + j) * B
                vec[plane.z, plane.x, h, j] = grad[:, at : at + B]
        grad_sum = TileSum([across_it, along_x, along_z], tr_small, slot0 + 2 * k * SUM_SLOTS, box.at[2 * k], 8)

        def beside_second(v, k=k):
            if v == 0:
                both = stacked(grad)
                grad_sum.put(pack(fold(dot(both, both, 1, 1))))
                grads[k] = grad
                if k:
                    conj[...] = direction
            if k == 0:
                rows_loop(*turned_later[v], 2, turn)

        gather_all(vec, plane, tr, beside_second)
        grad_sum.step()
        lax.fori_loop(0, 16, cut, 0)
        rows_loop(0, 40, UNROLL, forward(2 * N * k))
        grad_sum.step()
        rows_loop(40, ROWS, UNROLL, forward(2 * N * k))
        last = k + 1 == ITERS
        image_sum = TileSum(
            [in_plane, across_it] if last else [along_x, along_z, across_it],
            tr_small,
            slot0 + (2 * k + 1) * SUM_SLOTS,
            box.at[2 * k + 1],
            8 * (k + 1),
        )
        image_sum.put(image_grams(k))
        if not last:
            rows_loop(0, 40, UNROLL, backward(2 * N * k))
            small[k, GG] = unpack(grad_sum.take())
            image_sum.step()
            rows_loop(40, ROWS, UNROLL, backward(2 * N * k))
            add_up()
            image_sum.step()
        else:
            small[k, GG] = unpack(grad_sum.take())
            mix_of(k)
            image_sum.step()
            image_gram_of(k, image_sum.take())

    e2 = spd_solve(small[2, IG], small[2, GG])
    e1 = small[1, STEP] + exact(small[2, MIX], e2)
    e0 = small[0, STEP] + exact(small[1, MIX], e1)
    his, los = [], []
    for e in (e0, e1, e2):
        hi, lo = split(e.T)
        his += [hi, hi]
        los += [lo, lo]
    left = jnp.concatenate([jnp.concatenate(his, axis=1), jnp.concatenate(los, axis=1)], axis=0)
    out = dot(left, jnp.concatenate([stacked(grads[j]) for j in range(3)], axis=0), 1, 0)
    sol[...] = out[:N] + out[N:]
    width = 1024

    def strip(s, carry):
        at = pl.ds(pl.multiple_of(s * width, width), width)
        out = dot(left, images[:, at], 1, 0)
        res[:, at] = t_mem[:, at] - (out[:N] + out[N:])
        return carry

    lax.fori_loop(0, ROWS * B // width, strip, 0)
    tr_small.finish()


def body(blocks, block_cols, targets):
    n_row = lax.axis_size("row")
    n_col = lax.axis_size("col")
    group = CBD * n_row
    flat = block_cols.reshape(1, -1)
    table = order_of(flat // (CBD * n_col) * CBD + lax.rem(flat, CBD))
    vmem = pl.BlockSpec(memory_space=pltpu.VMEM)
    anywhere = pl.BlockSpec(memory_space=pl.ANY)
    width = CBD * B
    chunks = (4, 4, 2, CBD // 2, N, B)
    slots = RS_SLOTS + AG_SLOTS + 6 * SUM_SLOTS
    return tuple(
        pl.pallas_call(
            functools.partial(cgls_kernel, n_row, n_col),
            out_shape=[jax.ShapeDtypeStruct((N, width), F32), jax.ShapeDtypeStruct(targets.shape, F32)],
            in_specs=[pl.BlockSpec(memory_space=pltpu.SMEM), anywhere, anywhere],
            out_specs=[vmem] * 2,
            scratch_shapes=[
                pltpu.VMEM((ROWS, 2 * B, 4 * B), BF16),
                pltpu.VMEM((ROWS, 4 * B, 2 * B), BF16),
                pltpu.VMEM((ROWS * 4, N, B), F32),
                pltpu.VMEM((ROWS * 4, N, B), F32),
                pltpu.VMEM(chunks, F32),
                pltpu.VMEM(chunks, F32),
                pltpu.VMEM((group, 2 * N, B), BF16),
                pltpu.VMEM((2 * N * ITERS, ROWS * B), BF16),
                pltpu.VMEM((N, ROWS * B), F32),
                pltpu.VMEM((ITERS, N, width), F32),
                pltpu.VMEM((N, width), F32),
                pltpu.VMEM((2 * N, 2 * N * 4), F32),
                pltpu.VMEM((ITERS, 4, N, N), F32),
                pltpu.VMEM((2, 4, 6, 2, N, B), F32),
                pltpu.VMEM((2, 4, 4, N, B), F32),
                pltpu.VMEM((2, 6, 2, N, B), F32),
                pltpu.VMEM((6, 3, n_row, 24, B), F32),
                pltpu.SemaphoreType.DMA((slots,)),
                pltpu.SemaphoreType.DMA((slots,)),
                pltpu.SemaphoreType.DMA((SLOTS + 1,)),
            ],
            compiler_params=pltpu.CompilerParams(
                collective_id=0, has_side_effects=True, vmem_limit_bytes=60 * MIB
            ),
        )(table, blocks.reshape(-1, N, B), targets)
    )


def solution(mesh):
    placed = (P(("row", "col"), None, None, None), P(("row", "col"), None), P(None, ("row", "col")))
    return jax.shard_map(
        body,
        mesh=mesh,
        in_specs=placed,
        out_specs=(P(None, ("row", "col")), P(None, ("row", "col"))),
        check_vma=False,
    )
```

```python
import functools

import jax
import jax.numpy as jnp
from jax import lax
from jax.experimental import pallas as pl
from jax.experimental.pallas import tpu as pltpu
from jax.sharding import PartitionSpec as P

MESH = pl.DeviceIdType.MESH
F32 = jnp.float32
BF16 = jnp.bfloat16
ITERS = 3
CBD = 8
N = 32
B = 128
MIB = 2**20


def dot(a, b, ca, cb, precision=None):
    return lax.dot_general(
        a, b, (((ca,), (cb,)), ((), ())), precision=precision, preferred_element_type=F32
    )


def exact(a, b, ca=1, cb=0):
    return dot(a, b, ca, cb, lax.Precision.HIGHEST)


def split(x):
    hi = x.astype(BF16)
    lo = (x - hi.astype(F32)).astype(BF16)
    return hi, lo


def stacked(x):
    hi, lo = split(x)
    return jnp.concatenate([hi, lo], axis=0)


def pack(square):
    return jnp.concatenate([square[8 * g : 8 * g + 8] for g in range(4)], axis=1)


def unpack(tile):
    return jnp.concatenate([tile[:, N * g : N * g + N] for g in range(4)], axis=0)


def fold(square):
    half = square[:N] + square[N:]
    return half[:, :N] + half[:, N:]


def spd_solve(matrix, right):
    table = jnp.concatenate([matrix, right], axis=1)
    wide = (8, 2 * N)
    parts = [table[8 * g : 8 * g + 8] for g in range(4)]
    sub = lax.broadcasted_iota(jnp.int32, wide, 0)

    def lanes(group, b):
        return jnp.broadcast_to(group[:, b : b + 1], wide)

    def rows(group, a):
        return jnp.broadcast_to(group[a : a + 1], wide)

    for g in range(4):
        mine = parts[g]
        pivots = [lanes(mine, 8 * g + b) for b in range(8)]
        factors = [[lanes(parts[h], 8 * g + b) for b in range(8)] if h != g else None for h in range(4)]
        for a in range(8):
            inverse = 1.0 / rows(pivots[a], a)
            here = sub == a
            factor = pivots[a]
            for b in range(a + 1, 8):
                scaled = rows(pivots[b], a) * inverse
                pivots[b] = jnp.where(here, scaled, pivots[b] - factor * scaled)
            scaled = rows(mine, a) * inverse
            mine = jnp.where(here, scaled, mine - factor * scaled)
        parts[g] = mine
        for h in range(4):
            if h != g:
                for b in range(8):
                    parts[h] = parts[h] - factors[h][b] * rows(mine, b)
    return jnp.concatenate(parts, axis=0)[:, N : 2 * N]


def apply_t(square, both):
    hi, lo = split(square.T)
    left = jnp.concatenate([jnp.concatenate([hi, hi], axis=1), jnp.concatenate([lo, lo], axis=1)], axis=0)
    out = dot(left, both, 1, 0)
    return out[:N] + out[N:]


COL, ORDER, FIRST, LAST, SOME = range(5)


def order_kernel(cols, table):
    count = cols.shape[1]
    shape = (count, count)
    row = cols[...].astype(F32)
    across = jnp.broadcast_to(row, shape)
    down = across.T
    p = lax.broadcasted_iota(jnp.int32, shape, 0).astype(F32)
    q = lax.broadcasted_iota(jnp.int32, shape, 1).astype(F32)
    one = jnp.ones(shape, F32)
    zero = jnp.zeros(shape, F32)
    before = jnp.where((across < down) | ((across == down) & (q < p)), one, zero)
    twins = jnp.where((across == down) & (q < p), one, zero)
    rank = jnp.sum(before, axis=1, keepdims=True)
    alone = jnp.where(jnp.sum(twins, axis=1, keepdims=True) == 0.0, 1.0, 0.0)
    place = rank == q
    table[COL : COL + 1, :] = cols[...]
    table[ORDER : ORDER + 1, :] = jnp.sum(jnp.where(place, p, zero), axis=0, keepdims=True).astype(jnp.int32)
    table[FIRST : FIRST + 1, :] = jnp.sum(jnp.where(place, alone, zero), axis=0, keepdims=True).astype(jnp.int32)
    upto = jnp.sum(jnp.where(down <= q, one, zero), axis=0, keepdims=True)
    table[LAST : LAST + 1, :] = jnp.maximum(upto - 1.0, 0.0).astype(jnp.int32)
    some = jnp.sum(jnp.where(down == q, one, zero), axis=0, keepdims=True)
    table[SOME : SOME + 1, :] = jnp.where(some > 0.0, 1.0, 0.0).astype(jnp.int32)
    table[5:8, :] = jnp.zeros((3, count), jnp.int32)


def order_of(cols):
    return pl.pallas_call(
        order_kernel, out_shape=jax.ShapeDtypeStruct((8, cols.shape[1]), jnp.int32)
    )(cols)


class Traffic:
    def __init__(self, send_sem, recv_sem):
        self.send_sem, self.recv_sem = send_sem, recv_sem
        self.sent = []

    def send(self, slot, src, dst, device):
        copy = pltpu.make_async_remote_copy(
            src_ref=src,
            dst_ref=dst,
            send_sem=self.send_sem.at[slot],
            recv_sem=self.recv_sem.at[slot],
            device_id=device,
            device_id_type=MESH,
        )
        copy.start()
        self.sent.append(copy)
        return copy

    def finish(self):
        for copy in self.sent:
            copy.wait_send()
        self.sent = []


class Plane:
    def __init__(self, row, col):
        z, x = row // 4, lax.rem(row, 4)

        def along_x(d):
            return (z * 4 + lax.rem(x + d, 4), col)

        def along_z(d):
            return (lax.rem(z + d, 4) * 4 + x, col)

        self.z, self.x = z, x
        self.halves = ((x, z, along_x, along_z), (z, x, along_z, along_x))


def chunk(ref, h, ta, tb, s):
    zz, xx = (tb, ta) if h == 0 else (ta, tb)
    return ref.at[zz, xx, h] if s is None else ref.at[zz, xx, h, pl.ds(2 * s, 2)]


RS_SLOTS = 60
AG_SLOTS = 40
SUM_SLOTS = 22
OFFSETS = (2, 3, 1, 0)


def reduce_scatter(sums, plane, r1, p1, r2, tr, hook):
    c1, c2 = {}, {}
    halves = plane.halves

    def send1(u, h, idx):
        pa, pb, ring, _ = halves[h]
        tb = lax.rem(pb + OFFSETS[u], 4)
        off, s, d = ((2, 0, 1), (2, 1, 3), (1, 1, 1), (3, 0, 3))[idx]
        src = chunk(sums, h, lax.rem(pa + off, 4), tb, s)
        c1[u, h, idx] = tr.send((h * 4 + u) * 6 + idx, src, r1.at[h, u, idx], ring(d))

    def pass_on(u, h):
        pa, pb, ring, _ = halves[h]
        tb = lax.rem(pb + OFFSETS[u], 4)
        for idx, off, d in ((0, 1, 1), (1, 3, 3)):
            c1[u, h, idx].wait_recv()
            r1[h, u, idx] += chunk(sums, h, lax.rem(pa + off, 4), tb, idx)[...]
            c1[u, h, 4 + idx] = tr.send(
                (h * 4 + u) * 6 + 4 + idx, r1.at[h, u, idx], r1.at[h, u, 4 + idx], ring(d)
            )

    def send2(h, idx, src, d):
        c2[h, idx] = tr.send(48 + h * 6 + idx, src, r2.at[h, idx], halves[h][3](d))

    def close(u, h):
        pa, pb, _, _ = halves[h]
        tb = lax.rem(pb + OFFSETS[u], 4)
        for idx in (2, 3, 4, 5):
            c1[u, h, idx].wait_recv()
        p1[h, u, 0:2] = chunk(sums, h, pa, tb, 0)[...] + (r1[h, u, 3] + r1[h, u, 4])
        p1[h, u, 2:4] = chunk(sums, h, pa, tb, 1)[...] + (r1[h, u, 2] + r1[h, u, 5])
        if u == 0:
            send2(h, 0, p1.at[h, 0, pl.ds(0, 2)], 1)
            send2(h, 1, p1.at[h, 0, pl.ds(2, 2)], 3)
        if u == 1:
            send2(h, 3, p1.at[h, 1, pl.ds(0, 2)], 3)
            c2[h, 1].wait_recv()
            r2[h, 1] += p1[h, 1, 2:4]
            send2(h, 5, r2.at[h, 1], 3)
        if u == 2:
            send2(h, 2, p1.at[h, 2, pl.ds(2, 2)], 1)
            c2[h, 0].wait_recv()
            r2[h, 0] += p1[h, 2, 0:2]
            send2(h, 4, r2.at[h, 0], 1)

    both = range(2)
    for u in range(4):
        for h in both:
            send1(u, h, 0)
            send1(u, h, 1)
    def plain(u):
        for h in both:
            send1(u, h, 2)
            send1(u, h, 3)

    def on(u):
        for h in both:
            pass_on(u, h)

    def done(u):
        for h in both:
            close(u, h)

    plain(0)
    plain(1)
    hook(0)
    on(0)
    on(1)
    plain(2)
    plain(3)
    hook(1)
    on(2)
    done(0)
    on(3)
    done(1)
    done(2)
    done(3)
    hook(2)
    own = []
    for h in both:
        for idx in (2, 3, 4, 5):
            c2[h, idx].wait_recv()
        first = p1[h, 3, 0:2] + (r2[h, 3] + r2[h, 4])
        second = p1[h, 3, 2:4] + (r2[h, 2] + r2[h, 5])
        own += [first[0], first[1], second[0], second[1]]
    tr.finish()
    return jnp.concatenate(own, axis=1)


HOPS = ((0, None, 1), (0, None, 3), (3, 0, 1), (1, 1, 3))


def gather_all(vec, plane, tr, hook):
    halves = plane.halves
    order = (0, 3, 1, 2)
    c1, c2 = {}, {}

    def send1(h, idx):
        pa, pb, _, ring = halves[h]
        off, s, d = HOPS[idx]
        ref = chunk(vec, h, pa, lax.rem(pb + off, 4), s)
        c1[h, idx] = tr.send(RS_SLOTS + h * 4 + idx, ref, ref, ring(d))

    def send2(h, v, idx):
        pa, pb, ring, _ = halves[h]
        tb = lax.rem(pb + order[v], 4)
        off, s, d = HOPS[idx]
        ref = chunk(vec, h, lax.rem(pa + off, 4), tb, s)
        c2[h, v, idx] = tr.send(RS_SLOTS + 8 + (h * 4 + v) * 4 + idx, ref, ref, ring(d))

    both = range(2)

    def unit(v):
        for h in both:
            send2(h, v, 0)
            send2(h, v, 1)

    def pass_on(v):
        for h in both:
            for idx in range(2):
                c2[h, v, idx].wait_recv()
                send2(h, v, 2 + idx)

    for h in both:
        send1(h, 0)
        send1(h, 1)
    unit(0)
    hook(0)
    for h in both:
        for idx in range(2):
            c1[h, idx].wait_recv()
            send1(h, 2 + idx)
    unit(1)
    pass_on(0)
    unit(2)
    hook(1)
    for h in both:
        c1[h, 2].wait_recv()
        c1[h, 3].wait_recv()
    unit(3)
    pass_on(1)
    hook(2)
    pass_on(2)
    hook(3)
    pass_on(3)
    hook(4)
    for v in range(4):
        for h in both:
            c2[h, v, 2].wait_recv()
            c2[h, v, 3].wait_recv()
    tr.finish()


def sum_stages(row, col, n_row, n_col):
    z, x = row // 4, lax.rem(row, 4)
    along_x = ([(z * 4 + lax.rem(x + d, 4), col) for d in range(1, 4)], x, 4)
    along_z = ([(lax.rem(z + d, 4) * 4 + x, col) for d in range(1, 4)], z, 4)
    plane = ([(lax.rem(row + d, n_row), col) for d in range(1, n_row)], row, n_row)
    across = ([(row, lax.rem(col + d, n_col)) for d in range(1, n_col)], col, n_col)
    return along_x, along_z, plane, across


class TileSum:
    def __init__(self, stages, tr, slot, box, rows):
        self.stages, self.tr, self.slot, self.box, self.rows = stages, tr, slot, box, rows
        self.at, self.open = 0, []

    def put(self, tile):
        peers, me, _ = self.stages[self.at]
        ref = self.box.at[self.at, me, pl.ds(0, self.rows)]
        self.box[self.at, me, 0 : self.rows] = tile
        self.open = []
        for device in peers:
            self.open.append(self.tr.send(self.slot, ref, ref, device))
            self.slot += 1

    def take(self):
        for c in self.open:
            c.wait_recv()
        total = self.box[self.at, 0, 0 : self.rows]
        for i in range(1, self.stages[self.at][2]):
            total = total + self.box[self.at, i, 0 : self.rows]
        self.at += 1
        return total

    def step(self):
        self.put(self.take())


GG, IG, MIX, STEP = range(4)
ROWS = 64
UNROLL = 8
LEAD = UNROLL * B
LOAD = 4
SLOTS = 4


def rows_loop(lo, hi, width, step):
    def some(o, carry):
        for j in range(width):
            step(lo + o * width + j)
        return carry

    lax.fori_loop(0, (hi - lo) // width, some, 0)


def cgls_kernel(n_row, n_col, table, blocks, targets, sol, res, *scratch):
    across, down, pieces, running, sums, vec, parts, images, t_mem, grads = scratch[:10]
    conj, gram_acc, small, r1, p1, r2, box, send_sem, recv_sem, load_sem = scratch[10:]
    row, col = lax.axis_index("row"), lax.axis_index("col")
    plane = Plane(row, col)
    along_x, along_z, in_plane, across_it = sum_stages(row, col, n_row, n_col)
    tr, tr_small = Traffic(send_sem, recv_sem), Traffic(send_sem, recv_sem)

    size = LOAD * 16

    def load(step):
        slot = lax.rem(step, SLOTS)
        return pltpu.make_async_copy(
            blocks.at[pl.ds(step * size, size)], running.at[pl.ds(slot * size, size)], load_sem.at[slot]
        )

    read_targets = pltpu.make_async_copy(targets, t_mem, load_sem.at[SLOTS])
    read_targets.start()
    for s in range(SLOTS):
        load(s).start()

    barrier = pltpu.get_barrier_semaphore()
    who = in_plane[0] + across_it[0]
    for device in who:
        pl.semaphore_signal(barrier, inc=1, device_id=device, device_id_type=MESH)

    def lanes(i):
        return pl.ds(pl.multiple_of(i * B, B), B)

    def spot(i):
        return pl.ds(pl.multiple_of(LEAD + i * B, B), B)

    images[:, 0:LEAD] = jnp.zeros((2 * N * ITERS, LEAD), BF16)

    def piece(i, both, block):
        out = dot(jnp.concatenate([both, both], axis=1), block, 1, 0)
        out = out[:N] + out[N:]
        for k in range(4):
            pieces[i * 4 + k] = out[:, k * B : (k + 1) * B]

    read_targets.wait()

    def first(step, carry):
        load(step).wait()
        slot = lax.rem(step, SLOTS)
        for j in range(LOAD):
            i = step * LOAD + j
            his, los = [], []
            for k in range(4):
                base = slot * size + j * 16 + k * 4
                hi, lo = split(jnp.concatenate([running[base + q] for q in range(4)], axis=0))
                his.append(hi)
                los.append(lo)
            block = jnp.concatenate([jnp.concatenate(his, axis=1), jnp.concatenate(los, axis=1)], axis=0)
            across[i] = block
            piece(i, stacked(t_mem[:, lanes(i)]), block)

        @pl.when(step + SLOTS < ROWS // LOAD)
        def _():
            load(step + SLOTS).start()

        return carry

    lax.fori_loop(0, ROWS // LOAD, first, 0)

    def add_up():
        def run(o, total):
            for j in range(8):
                p = o * 8 + j
                total = jnp.where(table[FIRST, p] == 1, 0.0, total) + pieces[table[ORDER, p]]
                running[p] = total
            return total

        lax.fori_loop(0, ROWS * 4 // 8, run, jnp.zeros((N, B), F32))

        def pick(owner, carry):
            for h in range(2):
                for j in range(4):
                    c = owner * CBD + 4 * h + j
                    value = jnp.where(table[SOME, c] == 1, running[table[LAST, c]], 0.0)
                    sums[owner // 4, lax.rem(owner, 4), h, j] = value
            return carry

        lax.fori_loop(0, 16, pick, 0)

    def turn(i):
        for k in range(4):
            for h in range(2):
                tile = across[i, h * B : (h + 1) * B, k * B : (k + 1) * B]
                down[i, k * B : (k + 1) * B, h * B : (h + 1) * B] = tile.T

    def forward(at):
        def one(i):
            picked = jnp.concatenate([parts[table[COL, i * 4 + j]] for j in range(4)], axis=1)
            quad = dot(picked, down[i], 1, 0)
            quad = quad[:N] + quad[N:]
            images[at : at + 2 * N, spot(i)] = stacked(quad[:, :B] + quad[:, B:])

        return one

    def backward(at):
        def one(i):
            piece(i, images[at : at + 2 * N, spot(i)], across[i])

        return one

    def add_gram(k, group):
        at = pl.ds(pl.multiple_of(group * LEAD, LEAD), LEAD)
        mine = images[2 * N * k : 2 * N * (k + 1), at]
        gram_acc[:, 0 : 2 * N * (k + 1)] += dot(mine, images[0 : 2 * N * (k + 1), at], 1, 1)

    def forward_groups(k, lo, hi):
        row_of = forward(2 * N * k)

        def group(g, carry):
            add_gram(k, g)
            for j in range(UNROLL):
                row_of(g * UNROLL + j)
            return carry

        lax.fori_loop(lo, hi, group, 0)

    def image_grams(k):
        add_gram(k, ROWS // UNROLL)
        return jnp.concatenate(
            [pack(fold(gram_acc[:, 2 * N * j : 2 * N * (j + 1)])) for j in range(k, -1, -1)], axis=0
        )

    def mix_of(k):
        if k:
            small[k, MIX] = spd_solve(small[k - 1, GG], small[k, GG])

    def image_gram_of(k, total):
        gram = unpack(total[0:8])
        if k:
            mix = small[k, MIX]
            cross = unpack(total[8:16])
            if k == 2:
                cross = cross + exact(unpack(total[16:24]), small[1, MIX])
            mixed = exact(cross, mix)
            gram = gram + (mixed + mixed.T) + exact(mix, exact(small[k - 1, IG], mix), 0, 0)
        small[k, IG] = gram

    def cut(h, ta, tb):
        zz, xx = (tb, ta) if h == 0 else (ta, tb)
        for j in range(4):
            parts[(zz * 4 + xx) * CBD + 4 * h + j] = stacked(vec[zz, xx, h, j])

    def cut_unit(v, offsets):
        for h in range(2):
            pa, pb, _, _ = plane.halves[h]
            for off in offsets:
                cut(h, lax.rem(pa + off, 4), lax.rem(pb + (0, 3, 1, 2)[v], 4))

    add_up()
    pl.semaphore_wait(barrier, len(who))
    slot0 = RS_SLOTS + AG_SLOTS
    turned = {0: (0, 10), 1: (10, 22), 2: (22, 32)}
    turned_later = {0: (32, 36), 1: (36, 46), 2: (46, 52), 3: (52, 56), 4: (56, 64)}
    image_sum = None
    for k in range(ITERS):

        def beside_first(u, k=k):
            if k == 0:
                rows_loop(*turned[u], 2, turn)
            elif u == 0:
                mix_of(k - 1)
            elif u == 1:
                image_gram_of(k - 1, image_sum.take())
            else:
                small[k - 1, STEP] = spd_solve(small[k - 1, IG], small[k - 1, GG])

        fresh = reduce_scatter(sums, plane, r1, p1, r2, tr, beside_first)
        if k == 0:
            grad = fresh
        else:
            direction = fresh if k == 1 else fresh + apply_t(small[1, MIX], stacked(conj[...]))
            grad = grads[k - 1] - apply_t(small[k - 1, STEP], stacked(direction))
        for h in range(2):
            for j in range(4):
                at = (4 * h + j) * B
                vec[plane.z, plane.x, h, j] = grad[:, at : at + B]
        grad_sum = TileSum([across_it, along_x, along_z], tr_small, slot0 + 2 * k * SUM_SLOTS, box.at[2 * k], 8)

        def beside_second(v, k=k):
            if v == 0:
                both = stacked(grad)
                grad_sum.put(pack(fold(dot(both, both, 1, 1))))
                grads[k] = grad
                if k:
                    conj[...] = direction
            else:
                cut_unit(v - 1, (0, 1, 3))
            if k == 0:
                rows_loop(*turned_later[v], 2, turn)

        gather_all(vec, plane, tr, beside_second)
        grad_sum.step()
        for v in range(4):
            cut_unit(v, (2,))
        gram_acc[...] = jnp.zeros_like(gram_acc)
        forward_groups(k, 0, 5)
        grad_sum.step()
        forward_groups(k, 5, ROWS // UNROLL)
        last = k + 1 == ITERS
        image_sum = TileSum(
            [in_plane, across_it] if last else [along_x, along_z, across_it],
            tr_small,
            slot0 + (2 * k + 1) * SUM_SLOTS,
            box.at[2 * k + 1],
            8 * (k + 1),
        )
        image_sum.put(image_grams(k))
        if not last:
            rows_loop(0, 40, UNROLL, backward(2 * N * k))
            small[k, GG] = unpack(grad_sum.take())
            image_sum.step()
            rows_loop(40, ROWS, UNROLL, backward(2 * N * k))
            add_up()
            image_sum.step()
        else:
            small[k, GG] = unpack(grad_sum.take())
            mix_of(k)
            image_sum.step()
            image_gram_of(k, image_sum.take())

    e2 = spd_solve(small[2, IG], small[2, GG])
    e1 = small[1, STEP] + exact(small[2, MIX], e2)
    e0 = small[0, STEP] + exact(small[1, MIX], e1)
    his, los = [], []
    for e in (e0, e1, e2):
        hi, lo = split(e.T)
        his += [hi, hi]
        los += [lo, lo]
    left = jnp.concatenate([jnp.concatenate(his, axis=1), jnp.concatenate(los, axis=1)], axis=0)
    out = dot(left, jnp.concatenate([stacked(grads[j]) for j in range(3)], axis=0), 1, 0)
    sol[...] = out[:N] + out[N:]
    width = 1024

    def strip(s, carry):
        at = pl.ds(pl.multiple_of(s * width, width), width)
        out = dot(left, images[:, pl.ds(pl.multiple_of(LEAD + s * width, width), width)], 1, 0)
        res[:, at] = t_mem[:, at] - (out[:N] + out[N:])
        return carry

    lax.fori_loop(0, ROWS * B // width, strip, 0)
    tr_small.finish()


def body(blocks, block_cols, targets):
    n_row = lax.axis_size("row")
    n_col = lax.axis_size("col")
    group = CBD * n_row
    flat = block_cols.reshape(1, -1)
    table = order_of(flat // (CBD * n_col) * CBD + lax.rem(flat, CBD))
    vmem = pl.BlockSpec(memory_space=pltpu.VMEM)
    anywhere = pl.BlockSpec(memory_space=pl.ANY)
    width = CBD * B
    chunks = (4, 4, 2, CBD // 2, N, B)
    slots = RS_SLOTS + AG_SLOTS + 6 * SUM_SLOTS
    return tuple(
        pl.pallas_call(
            functools.partial(cgls_kernel, n_row, n_col),
            out_shape=[jax.ShapeDtypeStruct((N, width), F32), jax.ShapeDtypeStruct(targets.shape, F32)],
            in_specs=[pl.BlockSpec(memory_space=pltpu.SMEM), anywhere, anywhere],
            out_specs=[vmem] * 2,
            scratch_shapes=[
                pltpu.VMEM((ROWS, 2 * B, 4 * B), BF16),
                pltpu.VMEM((ROWS, 4 * B, 2 * B), BF16),
                pltpu.VMEM((ROWS * 4, N, B), F32),
                pltpu.VMEM((ROWS * 4, N, B), F32),
                pltpu.VMEM(chunks, F32),
                pltpu.VMEM(chunks, F32),
                pltpu.VMEM((group, 2 * N, B), BF16),
                pltpu.VMEM((2 * N * ITERS, LEAD + ROWS * B), BF16),
                pltpu.VMEM((N, ROWS * B), F32),
                pltpu.VMEM((ITERS, N, width), F32),
                pltpu.VMEM((N, width), F32),
                pltpu.VMEM((2 * N, 2 * N * 4), F32),
                pltpu.VMEM((ITERS, 4, N, N), F32),
                pltpu.VMEM((2, 4, 6, 2, N, B), F32),
                pltpu.VMEM((2, 4, 4, N, B), F32),
                pltpu.VMEM((2, 6, 2, N, B), F32),
                pltpu.VMEM((6, 3, n_row, 24, B), F32),
                pltpu.SemaphoreType.DMA((slots,)),
                pltpu.SemaphoreType.DMA((slots,)),
                pltpu.SemaphoreType.DMA((SLOTS + 1,)),
            ],
            compiler_params=pltpu.CompilerParams(
                collective_id=0, has_side_effects=True, vmem_limit_bytes=60 * MIB
            ),
        )(table, blocks.reshape(-1, N, B), targets)
    )


def solution(mesh):
    placed = (P(("row", "col"), None, None, None), P(("row", "col"), None), P(None, ("row", "col")))
    return jax.shard_map(
        body,
        mesh=mesh,
        in_specs=placed,
        out_specs=(P(None, ("row", "col")), P(None, ("row", "col"))),
        check_vma=False,
    )
```

```python
import functools

import jax
import jax.numpy as jnp
from jax import lax
from jax.experimental import pallas as pl
from jax.experimental.pallas import tpu as pltpu
from jax.sharding import PartitionSpec as P

MESH = pl.DeviceIdType.MESH
F32 = jnp.float32
BF16 = jnp.bfloat16
ITERS = 3
CBD = 8
N = 32
B = 128
MIB = 2**20


def dot(a, b, ca, cb, precision=None):
    return lax.dot_general(
        a, b, (((ca,), (cb,)), ((), ())), precision=precision, preferred_element_type=F32
    )


def exact(a, b, ca=1, cb=0):
    return dot(a, b, ca, cb, lax.Precision.HIGHEST)


def split(x):
    hi = x.astype(BF16)
    lo = (x - hi.astype(F32)).astype(BF16)
    return hi, lo


def stacked(x):
    hi, lo = split(x)
    return jnp.concatenate([hi, lo], axis=0)


def pack(square):
    return jnp.concatenate([square[8 * g : 8 * g + 8] for g in range(4)], axis=1)


def unpack(tile):
    return jnp.concatenate([tile[:, N * g : N * g + N] for g in range(4)], axis=0)


def fold(square):
    half = square[:N] + square[N:]
    return half[:, :N] + half[:, N:]


def spd_solve(matrix, right):
    table = jnp.concatenate([matrix, right], axis=1)
    wide = (8, 2 * N)
    parts = [table[8 * g : 8 * g + 8] for g in range(4)]
    sub = lax.broadcasted_iota(jnp.int32, wide, 0)

    def lanes(group, b):
        return jnp.broadcast_to(group[:, b : b + 1], wide)

    def rows(group, a):
        return jnp.broadcast_to(group[a : a + 1], wide)

    for g in range(4):
        mine = parts[g]
        pivots = [lanes(mine, 8 * g + b) for b in range(8)]
        factors = [[lanes(parts[h], 8 * g + b) for b in range(8)] if h != g else None for h in range(4)]
        for a in range(8):
            inverse = 1.0 / rows(pivots[a], a)
            here = sub == a
            factor = pivots[a]
            for b in range(a + 1, 8):
                scaled = rows(pivots[b], a) * inverse
                pivots[b] = jnp.where(here, scaled, pivots[b] - factor * scaled)
            scaled = rows(mine, a) * inverse
            mine = jnp.where(here, scaled, mine - factor * scaled)
        parts[g] = mine
        for h in range(4):
            if h != g:
                for b in range(8):
                    parts[h] = parts[h] - factors[h][b] * rows(mine, b)
    return jnp.concatenate(parts, axis=0)[:, N : 2 * N]


def left_of(squares):
    his, los = [], []
    for square in squares:
        hi, lo = split(square.T)
        his += [hi, hi]
        los += [lo, lo]
    return jnp.concatenate([jnp.concatenate(his, axis=1), jnp.concatenate(los, axis=1)], axis=0)


def halves_sum(left, both):
    out = dot(left, both, 1, 0)
    return out[:N] + out[N:]


COL, ORDER, FIRST, LAST, SOME = range(5)


def order_kernel(n_col, flat, table):
    count = flat.shape[1]
    cols = flat[...] // (CBD * n_col) * CBD + lax.rem(flat[...], CBD)
    shape = (count, count)
    row = cols.astype(F32)
    across = jnp.broadcast_to(row, shape)
    down = across.T
    p = lax.broadcasted_iota(jnp.int32, shape, 0).astype(F32)
    q = lax.broadcasted_iota(jnp.int32, shape, 1).astype(F32)
    one = jnp.ones(shape, F32)
    zero = jnp.zeros(shape, F32)
    before = jnp.where((across < down) | ((across == down) & (q < p)), one, zero)
    twins = jnp.where((across == down) & (q < p), one, zero)
    rank = jnp.sum(before, axis=1, keepdims=True)
    alone = jnp.where(jnp.sum(twins, axis=1, keepdims=True) == 0.0, 1.0, 0.0)
    place = rank == q
    table[COL : COL + 1, :] = cols
    table[ORDER : ORDER + 1, :] = jnp.sum(jnp.where(place, p, zero), axis=0, keepdims=True).astype(jnp.int32)
    table[FIRST : FIRST + 1, :] = jnp.sum(jnp.where(place, alone, zero), axis=0, keepdims=True).astype(jnp.int32)
    upto = jnp.sum(jnp.where(down <= q, one, zero), axis=0, keepdims=True)
    table[LAST : LAST + 1, :] = jnp.maximum(upto - 1.0, 0.0).astype(jnp.int32)
    some = jnp.sum(jnp.where(down == q, one, zero), axis=0, keepdims=True)
    table[SOME : SOME + 1, :] = jnp.where(some > 0.0, 1.0, 0.0).astype(jnp.int32)
    table[5:8, :] = jnp.zeros((3, count), jnp.int32)


def order_of(flat, n_col):
    return pl.pallas_call(
        functools.partial(order_kernel, n_col),
        out_shape=jax.ShapeDtypeStruct((8, flat.shape[1]), jnp.int32),
    )(flat)


class Traffic:
    def __init__(self, send_sem, recv_sem):
        self.send_sem, self.recv_sem = send_sem, recv_sem
        self.sent = []

    def send(self, slot, src, dst, device):
        copy = pltpu.make_async_remote_copy(
            src_ref=src,
            dst_ref=dst,
            send_sem=self.send_sem.at[slot],
            recv_sem=self.recv_sem.at[slot],
            device_id=device,
            device_id_type=MESH,
        )
        copy.start()
        self.sent.append(copy)
        return copy

    def finish(self):
        for copy in self.sent:
            copy.wait_send()
        self.sent = []


class Plane:
    def __init__(self, row, col):
        z, x = row // 4, lax.rem(row, 4)

        def along_x(d):
            return (z * 4 + lax.rem(x + d, 4), col)

        def along_z(d):
            return (lax.rem(z + d, 4) * 4 + x, col)

        self.z, self.x = z, x
        self.halves = ((x, z, along_x, along_z), (z, x, along_z, along_x))


def chunk(ref, h, ta, tb, s):
    zz, xx = (tb, ta) if h == 0 else (ta, tb)
    return ref.at[zz, xx, h] if s is None else ref.at[zz, xx, h, pl.ds(2 * s, 2)]


RS_SLOTS = 60
AG_SLOTS = 40
SUM_SLOTS = 22
OFFSETS = (2, 3, 1, 0)


def reduce_scatter(sums, plane, r1, p1, r2, tr, hook):
    c1, c2 = {}, {}
    halves = plane.halves

    def send1(u, h, idx):
        pa, pb, ring, _ = halves[h]
        tb = lax.rem(pb + OFFSETS[u], 4)
        off, s, d = ((2, 0, 1), (2, 1, 3), (1, 1, 1), (3, 0, 3))[idx]
        src = chunk(sums, h, lax.rem(pa + off, 4), tb, s)
        c1[u, h, idx] = tr.send((h * 4 + u) * 6 + idx, src, r1.at[h, u, idx], ring(d))

    def pass_on(u, h):
        pa, pb, ring, _ = halves[h]
        tb = lax.rem(pb + OFFSETS[u], 4)
        for idx, off, d in ((0, 1, 1), (1, 3, 3)):
            c1[u, h, idx].wait_recv()
            r1[h, u, idx] += chunk(sums, h, lax.rem(pa + off, 4), tb, idx)[...]
            c1[u, h, 4 + idx] = tr.send(
                (h * 4 + u) * 6 + 4 + idx, r1.at[h, u, idx], r1.at[h, u, 4 + idx], ring(d)
            )

    def send2(h, idx, src, d):
        c2[h, idx] = tr.send(48 + h * 6 + idx, src, r2.at[h, idx], halves[h][3](d))

    def close(u, h):
        pa, pb, _, _ = halves[h]
        tb = lax.rem(pb + OFFSETS[u], 4)
        for idx in (2, 3, 4, 5):
            c1[u, h, idx].wait_recv()
        p1[h, u, 0:2] = chunk(sums, h, pa, tb, 0)[...] + (r1[h, u, 3] + r1[h, u, 4])
        p1[h, u, 2:4] = chunk(sums, h, pa, tb, 1)[...] + (r1[h, u, 2] + r1[h, u, 5])
        if u == 0:
            send2(h, 0, p1.at[h, 0, pl.ds(0, 2)], 1)
            send2(h, 1, p1.at[h, 0, pl.ds(2, 2)], 3)
        if u == 1:
            send2(h, 3, p1.at[h, 1, pl.ds(0, 2)], 3)
            c2[h, 1].wait_recv()
            r2[h, 1] += p1[h, 1, 2:4]
            send2(h, 5, r2.at[h, 1], 3)
        if u == 2:
            send2(h, 2, p1.at[h, 2, pl.ds(2, 2)], 1)
            c2[h, 0].wait_recv()
            r2[h, 0] += p1[h, 2, 0:2]
            send2(h, 4, r2.at[h, 0], 1)

    both = range(2)
    for u in range(4):
        for h in both:
            send1(u, h, 0)
            send1(u, h, 1)
    def plain(u):
        for h in both:
            send1(u, h, 2)
            send1(u, h, 3)

    def on(u):
        for h in both:
            pass_on(u, h)

    def done(u):
        for h in both:
            close(u, h)

    plain(0)
    plain(1)
    hook(0)
    on(0)
    on(1)
    plain(2)
    plain(3)
    hook(1)
    on(2)
    done(0)
    on(3)
    done(1)
    done(2)
    done(3)
    hook(2)
    own = []
    for h in both:
        for idx in (2, 3, 4, 5):
            c2[h, idx].wait_recv()
        first = p1[h, 3, 0:2] + (r2[h, 3] + r2[h, 4])
        second = p1[h, 3, 2:4] + (r2[h, 2] + r2[h, 5])
        own += [first[0], first[1], second[0], second[1]]
    tr.finish()
    return jnp.concatenate(own, axis=1)


HOPS = ((0, None, 1), (0, None, 3), (3, 0, 1), (1, 1, 3))


def gather_all(vec, plane, tr, hook):
    halves = plane.halves
    order = (0, 3, 1, 2)
    c1, c2 = {}, {}

    def send1(h, idx):
        pa, pb, _, ring = halves[h]
        off, s, d = HOPS[idx]
        ref = chunk(vec, h, pa, lax.rem(pb + off, 4), s)
        c1[h, idx] = tr.send(RS_SLOTS + h * 4 + idx, ref, ref, ring(d))

    def send2(h, v, idx):
        pa, pb, ring, _ = halves[h]
        tb = lax.rem(pb + order[v], 4)
        off, s, d = HOPS[idx]
        ref = chunk(vec, h, lax.rem(pa + off, 4), tb, s)
        c2[h, v, idx] = tr.send(RS_SLOTS + 8 + (h * 4 + v) * 4 + idx, ref, ref, ring(d))

    both = range(2)

    def unit(v):
        for h in both:
            send2(h, v, 0)
            send2(h, v, 1)

    def pass_on(v):
        for h in both:
            for idx in range(2):
                c2[h, v, idx].wait_recv()
                send2(h, v, 2 + idx)

    for h in both:
        send1(h, 0)
        send1(h, 1)
    unit(0)
    hook(0)
    for h in both:
        for idx in range(2):
            c1[h, idx].wait_recv()
            send1(h, 2 + idx)
    unit(1)
    pass_on(0)
    unit(2)
    hook(1)
    for h in both:
        c1[h, 2].wait_recv()
        c1[h, 3].wait_recv()
    unit(3)
    pass_on(1)
    hook(2)
    pass_on(2)
    hook(3)
    pass_on(3)
    hook(4)
    for v in range(4):
        for h in both:
            c2[h, v, 2].wait_recv()
            c2[h, v, 3].wait_recv()
    tr.finish()


def sum_stages(row, col, n_row, n_col):
    z, x = row // 4, lax.rem(row, 4)
    along_x = ([(z * 4 + lax.rem(x + d, 4), col) for d in range(1, 4)], x, 4)
    along_z = ([(lax.rem(z + d, 4) * 4 + x, col) for d in range(1, 4)], z, 4)
    plane = ([(lax.rem(row + d, n_row), col) for d in range(1, n_row)], row, n_row)
    across = ([(row, lax.rem(col + d, n_col)) for d in range(1, n_col)], col, n_col)
    return along_x, along_z, plane, across


class TileSum:
    def __init__(self, stages, tr, slot, box, rows):
        self.stages, self.tr, self.slot, self.box, self.rows = stages, tr, slot, box, rows
        self.at, self.open = 0, []

    def put(self, tile):
        peers, me, _ = self.stages[self.at]
        ref = self.box.at[self.at, me, pl.ds(0, self.rows)]
        self.box[self.at, me, 0 : self.rows] = tile
        self.open = []
        for device in peers:
            self.open.append(self.tr.send(self.slot, ref, ref, device))
            self.slot += 1

    def take(self):
        for c in self.open:
            c.wait_recv()
        total = self.box[self.at, 0, 0 : self.rows]
        for i in range(1, self.stages[self.at][2]):
            total = total + self.box[self.at, i, 0 : self.rows]
        self.at += 1
        return total

    def step(self):
        self.put(self.take())


GG, IG, MIX, STEP = range(4)
ROWS = 64
UNROLL = 8
LEAD = UNROLL * B
LOAD = 4
SLOTS = 4


def rows_loop(lo, hi, width, step):
    def some(o, carry):
        for j in range(width):
            step(lo + o * width + j)
        return carry

    lax.fori_loop(0, (hi - lo) // width, some, 0)


def cgls_kernel(n_row, n_col, table, blocks, targets, sol, res, *scratch):
    across, down, pieces, running, sums, vec, parts, images, t_mem, grads = scratch[:10]
    conj, gram_acc, small, r1, p1, r2, box, last_box, send_sem, recv_sem, load_sem, out_sem = scratch[10:]
    row, col = lax.axis_index("row"), lax.axis_index("col")
    plane = Plane(row, col)
    along_x, along_z, in_plane, across_it = sum_stages(row, col, n_row, n_col)
    tr, tr_small = Traffic(send_sem, recv_sem), Traffic(send_sem, recv_sem)

    size = LOAD * 16

    def load(step):
        slot = lax.rem(step, SLOTS)
        return pltpu.make_async_copy(
            blocks.at[pl.ds(step * size, size)], running.at[pl.ds(slot * size, size)], load_sem.at[slot]
        )

    read_targets = pltpu.make_async_copy(targets, t_mem, load_sem.at[SLOTS])
    read_targets.start()
    for s in range(SLOTS):
        load(s).start()

    barrier = pltpu.get_barrier_semaphore()
    who = in_plane[0] + across_it[0]
    for device in who:
        pl.semaphore_signal(barrier, inc=1, device_id=device, device_id_type=MESH)

    def lanes(i):
        return pl.ds(pl.multiple_of(i * B, B), B)

    def spot(i):
        return pl.ds(pl.multiple_of(LEAD + i * B, B), B)

    images[:, 0:LEAD] = jnp.zeros((2 * N * ITERS, LEAD), BF16)

    def piece(i, both, block):
        out = dot(jnp.concatenate([both, both], axis=1), block, 1, 0)
        out = out[:N] + out[N:]
        for k in range(4):
            pieces[i * 4 + k] = out[:, k * B : (k + 1) * B]

    read_targets.wait()

    def first(step, carry):
        load(step).wait()
        slot = lax.rem(step, SLOTS)
        for j in range(LOAD):
            i = step * LOAD + j
            his, los = [], []
            for k in range(4):
                base = slot * size + j * 16 + k * 4
                hi, lo = split(jnp.concatenate([running[base + q] for q in range(4)], axis=0))
                his.append(hi)
                los.append(lo)
            block = jnp.concatenate([jnp.concatenate(his, axis=1), jnp.concatenate(los, axis=1)], axis=0)
            across[i] = block
            piece(i, stacked(t_mem[:, lanes(i)]), block)

        @pl.when(step + SLOTS < ROWS // LOAD)
        def _():
            load(step + SLOTS).start()

        return carry

    lax.fori_loop(0, ROWS // LOAD, first, 0)

    def add_up():
        def run(o, total):
            for j in range(8):
                p = o * 8 + j
                total = jnp.where(table[FIRST, p] == 1, 0.0, total) + pieces[table[ORDER, p]]
                running[p] = total
            return total

        lax.fori_loop(0, ROWS * 4 // 8, run, jnp.zeros((N, B), F32))

        def pick(owner, carry):
            for h in range(2):
                for j in range(4):
                    c = owner * CBD + 4 * h + j
                    value = jnp.where(table[SOME, c] == 1, running[table[LAST, c]], 0.0)
                    sums[owner // 4, lax.rem(owner, 4), h, j] = value
            return carry

        lax.fori_loop(0, 16, pick, 0)

    def turn(i):
        for k in range(4):
            for h in range(2):
                tile = across[i, h * B : (h + 1) * B, k * B : (k + 1) * B]
                down[i, k * B : (k + 1) * B, h * B : (h + 1) * B] = tile.T

    def forward(at):
        def one(i):
            picked = jnp.concatenate([parts[table[COL, i * 4 + j]] for j in range(4)], axis=1)
            quad = dot(picked, down[i], 1, 0)
            quad = quad[:N] + quad[N:]
            images[at : at + 2 * N, spot(i)] = stacked(quad[:, :B] + quad[:, B:])

        return one

    def backward(at):
        def one(i):
            piece(i, images[at : at + 2 * N, spot(i)], across[i])

        return one

    def add_gram(k, group):
        at = pl.ds(pl.multiple_of(group * LEAD, LEAD), LEAD)
        mine = images[2 * N * k : 2 * N * (k + 1), at]
        gram_acc[:, 0 : 2 * N * (k + 1)] += dot(mine, images[0 : 2 * N * (k + 1), at], 1, 1)

    def forward_groups(k, lo, hi):
        row_of = forward(2 * N * k)

        def group(g, carry):
            add_gram(k, g)
            for j in range(UNROLL):
                row_of(g * UNROLL + j)
            return carry

        lax.fori_loop(lo, hi, group, 0)

    def image_grams(k):
        add_gram(k, ROWS // UNROLL)
        return jnp.concatenate(
            [pack(fold(gram_acc[:, 2 * N * j : 2 * N * (j + 1)])) for j in range(k, -1, -1)], axis=0
        )

    def mix_of(k):
        if k:
            small[k, MIX] = spd_solve(small[k - 1, GG], small[k, GG])

    def image_gram_of(k, total):
        gram = unpack(total[0:8])
        if k:
            mix = small[k, MIX]
            cross = unpack(total[8:16])
            if k == 2:
                cross = cross + exact(unpack(total[16:24]), small[1, MIX])
            mixed = exact(cross, mix)
            gram = gram + (mixed + mixed.T) + exact(mix, exact(small[k - 1, IG], mix), 0, 0)
        small[k, IG] = gram

    def cut(h, ta, tb):
        zz, xx = (tb, ta) if h == 0 else (ta, tb)
        for j in range(4):
            parts[(zz * 4 + xx) * CBD + 4 * h + j] = stacked(vec[zz, xx, h, j])

    def cut_unit(v, offsets):
        for h in range(2):
            pa, pb, _, _ = plane.halves[h]
            for off in offsets:
                cut(h, lax.rem(pa + off, 4), lax.rem(pb + (0, 3, 1, 2)[v], 4))

    add_up()
    pl.semaphore_wait(barrier, len(who))
    slot0 = RS_SLOTS + AG_SLOTS
    width = 1024
    strips = ROWS * B // width
    turned = {0: (0, 10), 1: (10, 22), 2: (22, 32)}
    turned_later = {0: (32, 36), 1: (36, 46), 2: (46, 52), 3: (52, 56), 4: (56, 64)}
    image_sum = None
    for k in range(ITERS):

        ready = []

        def beside_first(u, k=k, ready=ready):
            if k == 0:
                rows_loop(*turned[u], 2, turn)
            elif u == 0:
                mix_of(k - 1)
            elif u == 1:
                image_gram_of(k - 1, image_sum.take())
            else:
                step = spd_solve(small[k - 1, IG], small[k - 1, GG])
                small[k - 1, STEP] = step
                left = left_of([step])
                ready.append(left)
                if k == 1:
                    ready.append(grads[0])
                else:
                    known = halves_sum(left_of([small[1, MIX]]), stacked(conj[...]))
                    ready.append(grads[1] - halves_sum(left, stacked(known)))

        fresh = reduce_scatter(sums, plane, r1, p1, r2, tr, beside_first)
        if k == 0:
            grad = fresh
        else:
            grad = ready[1] - halves_sum(ready[0], stacked(fresh))
        for h in range(2):
            for j in range(4):
                at = (4 * h + j) * B
                vec[plane.z, plane.x, h, j] = grad[:, at : at + B]
        grad_sum = TileSum([across_it, along_x, along_z], tr_small, slot0 + 2 * k * SUM_SLOTS, box.at[2 * k], 8)

        def beside_second(v, k=k):
            if v == 0:
                both = stacked(grad)
                grad_sum.put(pack(fold(dot(both, both, 1, 1))))
                grads[k] = grad
                if k == 1:
                    conj[...] = fresh
            else:
                cut_unit(v - 1, (0, 1, 3))
            if k == 0:
                rows_loop(*turned_later[v], 2, turn)

        gather_all(vec, plane, tr, beside_second)
        grad_sum.step()
        for v in range(4):
            cut_unit(v, (2,))
        gram_acc[...] = jnp.zeros_like(gram_acc)
        forward_groups(k, 0, 5)
        grad_sum.step()
        forward_groups(k, 5, ROWS // UNROLL)
        last = k + 1 == ITERS
        image_sum = TileSum(
            [in_plane, across_it] if last else [along_x, along_z, across_it],
            tr_small,
            slot0 + (2 * k + 1) * SUM_SLOTS,
            last_box if last else box.at[2 * k + 1],
            8 * (k + 1),
        )
        image_sum.put(image_grams(k))
        if not last:
            rows_loop(0, 40, UNROLL, backward(2 * N * k))
            small[k, GG] = unpack(grad_sum.take())
            image_sum.step()
            rows_loop(40, ROWS, UNROLL, backward(2 * N * k))
            add_up()
            image_sum.step()
        else:
            small[k, GG] = unpack(grad_sum.take())
            mix_of(k)
            mix = small[2, MIX]
            now = small[1, STEP]
            ahead = [exact(small[1, MIX], mix), mix]
            upto = [small[0, STEP] + exact(small[1, MIX], now), now]
            left = jnp.concatenate([left_of(ahead), left_of(upto)], axis=0)
            out = dot(left, jnp.concatenate([stacked(grads[j]) for j in range(2)], axis=0), 1, 0)
            grads[2] = grads[2] + (out[:N] + out[N : 2 * N])
            conj[...] = out[2 * N : 3 * N] + out[3 * N :]

            def prepare(s, carry, left=left):
                at = pl.ds(pl.multiple_of(s * width, width), width)
                there = pl.ds(pl.multiple_of(LEAD + s * width, width), width)
                out = dot(left, images[0 : 4 * N, there], 1, 0)
                own = images[4 * N : 5 * N, there].astype(F32) + images[5 * N : 6 * N, there].astype(F32)
                images[4 * N : 6 * N, there] = stacked(own + (out[:N] + out[N : 2 * N]))
                t_mem[:, at] = t_mem[:, at] - (out[2 * N : 3 * N] + out[3 * N :])
                return carry

            lax.fori_loop(0, ROWS * B // width, prepare, 0)
            image_sum.step()
            image_gram_of(k, image_sum.take())

    left = left_of([spd_solve(small[2, IG], small[2, GG])])
    conj[...] = conj[...] + halves_sum(left, stacked(grads[2]))
    out_sol = pltpu.make_async_copy(conj, sol, out_sem.at[strips])
    out_sol.start()

    def write(s):
        at = pl.ds(pl.multiple_of(s * width, width), width)
        return pltpu.make_async_copy(t_mem.at[:, at], res.at[:, at], out_sem.at[s])

    def finish(s, carry):
        at = pl.ds(pl.multiple_of(s * width, width), width)
        there = pl.ds(pl.multiple_of(LEAD + s * width, width), width)
        t_mem[:, at] = t_mem[:, at] - halves_sum(left, images[4 * N : 6 * N, there])
        write(s).start()
        return carry

    lax.fori_loop(0, strips, finish, 0)
    out_sol.wait()

    def wait(s, carry):
        write(s).wait()
        return carry

    lax.fori_loop(0, strips, wait, 0)
    tr_small.finish()


def body(blocks, block_cols, targets):
    n_row = lax.axis_size("row")
    n_col = lax.axis_size("col")
    group = CBD * n_row
    table = order_of(block_cols.reshape(1, -1), n_col)
    anywhere = pl.BlockSpec(memory_space=pl.ANY)
    width = CBD * B
    chunks = (4, 4, 2, CBD // 2, N, B)
    slots = RS_SLOTS + AG_SLOTS + 6 * SUM_SLOTS
    return tuple(
        pl.pallas_call(
            functools.partial(cgls_kernel, n_row, n_col),
            out_shape=[jax.ShapeDtypeStruct((N, width), F32), jax.ShapeDtypeStruct(targets.shape, F32)],
            in_specs=[pl.BlockSpec(memory_space=pltpu.SMEM), anywhere, anywhere],
            out_specs=[anywhere] * 2,
            scratch_shapes=[
                pltpu.VMEM((ROWS, 2 * B, 4 * B), BF16),
                pltpu.VMEM((ROWS, 4 * B, 2 * B), BF16),
                pltpu.VMEM((ROWS * 4, N, B), F32),
                pltpu.VMEM((ROWS * 4, N, B), F32),
                pltpu.VMEM(chunks, F32),
                pltpu.VMEM(chunks, F32),
                pltpu.VMEM((group, 2 * N, B), BF16),
                pltpu.VMEM((2 * N * ITERS, LEAD + ROWS * B), BF16),
                pltpu.VMEM((N, ROWS * B), F32),
                pltpu.VMEM((ITERS, N, width), F32),
                pltpu.VMEM((N, width), F32),
                pltpu.VMEM((2 * N, 2 * N * 4), F32),
                pltpu.VMEM((ITERS, 4, N, N), F32),
                pltpu.VMEM((2, 4, 6, 2, N, B), F32),
                pltpu.VMEM((2, 4, 4, N, B), F32),
                pltpu.VMEM((2, 6, 2, N, B), F32),
                pltpu.VMEM((5, 3, n_col, 16, B), F32),
                pltpu.VMEM((2, n_row, 24, B), F32),
                pltpu.SemaphoreType.DMA((slots,)),
                pltpu.SemaphoreType.DMA((slots,)),
                pltpu.SemaphoreType.DMA((SLOTS + 1,)),
                pltpu.SemaphoreType.DMA((ROWS * B // 1024 + 1,)),
            ],
            compiler_params=pltpu.CompilerParams(
                collective_id=0, has_side_effects=True, vmem_limit_bytes=60 * MIB
            ),
        )(table, blocks.reshape(-1, N, B), targets)
    )


def solution(mesh):
    placed = (P(("row", "col"), None, None, None), P(("row", "col"), None), P(None, ("row", "col")))
    return jax.shard_map(
        body,
        mesh=mesh,
        in_specs=placed,
        out_specs=(P(None, ("row", "col")), P(None, ("row", "col"))),
        check_vma=False,
    )
```

```python
import functools

import jax
import jax.numpy as jnp
from jax import lax
from jax.experimental import pallas as pl
from jax.experimental.pallas import tpu as pltpu
from jax.sharding import PartitionSpec as P

MESH = pl.DeviceIdType.MESH
F32 = jnp.float32
BF16 = jnp.bfloat16
ITERS = 3
CBD = 8
N = 32
B = 128
MIB = 2**20


def dot(a, b, ca, cb, precision=None):
    return lax.dot_general(
        a, b, (((ca,), (cb,)), ((), ())), precision=precision, preferred_element_type=F32
    )


def exact(a, b, ca=1, cb=0):
    return dot(a, b, ca, cb, lax.Precision.HIGHEST)


def split(x):
    hi = x.astype(BF16)
    lo = (x - hi.astype(F32)).astype(BF16)
    return hi, lo


def stacked(x):
    hi, lo = split(x)
    return jnp.concatenate([hi, lo], axis=0)


def pack(square):
    return jnp.concatenate([square[8 * g : 8 * g + 8] for g in range(4)], axis=1)


def unpack(tile):
    return jnp.concatenate([tile[:, N * g : N * g + N] for g in range(4)], axis=0)


def fold(square):
    half = square[:N] + square[N:]
    return half[:, :N] + half[:, N:]


def spd_solve(matrix, right):
    table = jnp.concatenate([matrix, right], axis=1)
    wide = (8, 2 * N)
    parts = [table[8 * g : 8 * g + 8] for g in range(4)]
    sub = lax.broadcasted_iota(jnp.int32, wide, 0)

    def lanes(group, b):
        return jnp.broadcast_to(group[:, b : b + 1], wide)

    def rows(group, a):
        return jnp.broadcast_to(group[a : a + 1], wide)

    for g in range(4):
        mine = parts[g]
        pivots = [lanes(mine, 8 * g + b) for b in range(8)]
        factors = [[lanes(parts[h], 8 * g + b) for b in range(8)] if h != g else None for h in range(4)]
        for a in range(8):
            inverse = 1.0 / rows(pivots[a], a)
            here = sub == a
            factor = pivots[a]
            for b in range(a + 1, 8):
                scaled = rows(pivots[b], a) * inverse
                pivots[b] = jnp.where(here, scaled, pivots[b] - factor * scaled)
            scaled = rows(mine, a) * inverse
            mine = jnp.where(here, scaled, mine - factor * scaled)
        parts[g] = mine
        for h in range(4):
            if h != g:
                for b in range(8):
                    parts[h] = parts[h] - factors[h][b] * rows(mine, b)
    return jnp.concatenate(parts, axis=0)[:, N : 2 * N]


def left_of(squares):
    his, los = [], []
    for square in squares:
        hi, lo = split(square.T)
        his += [hi, hi]
        los += [lo, lo]
    return jnp.concatenate([jnp.concatenate(his, axis=1), jnp.concatenate(los, axis=1)], axis=0)


def halves_sum(left, both):
    out = dot(left, both, 1, 0)
    return out[:N] + out[N:]


COL, ORDER, FIRST, LAST, SOME = range(5)


def order_kernel(n_col, flat, table):
    count = flat.shape[1]
    cols = flat[...] // (CBD * n_col) * CBD + lax.rem(flat[...], CBD)
    shape = (count, count)
    row = cols.astype(F32)
    across = jnp.broadcast_to(row, shape)
    down = across.T
    p = lax.broadcasted_iota(jnp.int32, shape, 0).astype(F32)
    q = lax.broadcasted_iota(jnp.int32, shape, 1).astype(F32)
    one = jnp.ones(shape, F32)
    zero = jnp.zeros(shape, F32)
    before = jnp.where((across < down) | ((across == down) & (q < p)), one, zero)
    twins = jnp.where((across == down) & (q < p), one, zero)
    rank = jnp.sum(before, axis=1, keepdims=True)
    alone = jnp.where(jnp.sum(twins, axis=1, keepdims=True) == 0.0, 1.0, 0.0)
    place = rank == q
    table[COL : COL + 1, :] = cols
    table[ORDER : ORDER + 1, :] = jnp.sum(jnp.where(place, p, zero), axis=0, keepdims=True).astype(jnp.int32)
    table[FIRST : FIRST + 1, :] = jnp.sum(jnp.where(place, alone, zero), axis=0, keepdims=True).astype(jnp.int32)
    upto = jnp.sum(jnp.where(down <= q, one, zero), axis=0, keepdims=True)
    table[LAST : LAST + 1, :] = jnp.maximum(upto - 1.0, 0.0).astype(jnp.int32)
    some = jnp.sum(jnp.where(down == q, one, zero), axis=0, keepdims=True)
    table[SOME : SOME + 1, :] = jnp.where(some > 0.0, 1.0, 0.0).astype(jnp.int32)
    table[5:8, :] = jnp.zeros((3, count), jnp.int32)


def order_of(flat, n_col):
    return pl.pallas_call(
        functools.partial(order_kernel, n_col),
        out_shape=jax.ShapeDtypeStruct((8, flat.shape[1]), jnp.int32),
    )(flat)


class Traffic:
    def __init__(self, send_sem, recv_sem):
        self.send_sem, self.recv_sem = send_sem, recv_sem
        self.sent = []

    def send(self, slot, src, dst, device):
        copy = pltpu.make_async_remote_copy(
            src_ref=src,
            dst_ref=dst,
            send_sem=self.send_sem.at[slot],
            recv_sem=self.recv_sem.at[slot],
            device_id=device,
            device_id_type=MESH,
        )
        copy.start()
        self.sent.append(copy)
        return copy

    def finish(self):
        for copy in self.sent:
            copy.wait_send()
        self.sent = []


class Plane:
    def __init__(self, row, col):
        z, x = row // 4, lax.rem(row, 4)

        def along_x(d):
            return (z * 4 + lax.rem(x + d, 4), col)

        def along_z(d):
            return (lax.rem(z + d, 4) * 4 + x, col)

        self.z, self.x = z, x
        self.halves = ((x, z, along_x, along_z), (z, x, along_z, along_x))


def chunk(ref, h, ta, tb, s):
    zz, xx = (tb, ta) if h == 0 else (ta, tb)
    return ref.at[zz, xx, h] if s is None else ref.at[zz, xx, h, pl.ds(2 * s, 2)]


RS_SLOTS = 60
AG_SLOTS = 40
SUM_SLOTS = 22
OFFSETS = (2, 3, 1, 0)


def reduce_scatter(sums, plane, r1, p1, r2, tr, hook):
    c1, c2 = {}, {}
    halves = plane.halves

    def send1(u, h, idx):
        pa, pb, ring, _ = halves[h]
        tb = lax.rem(pb + OFFSETS[u], 4)
        off, s, d = ((2, 0, 1), (2, 1, 3), (1, 1, 1), (3, 0, 3))[idx]
        src = chunk(sums, h, lax.rem(pa + off, 4), tb, s)
        c1[u, h, idx] = tr.send((h * 4 + u) * 6 + idx, src, r1.at[h, u, idx], ring(d))

    def pass_on(u, h):
        pa, pb, ring, _ = halves[h]
        tb = lax.rem(pb + OFFSETS[u], 4)
        for idx, off, d in ((0, 1, 1), (1, 3, 3)):
            c1[u, h, idx].wait_recv()
            r1[h, u, idx] += chunk(sums, h, lax.rem(pa + off, 4), tb, idx)[...]
            c1[u, h, 4 + idx] = tr.send(
                (h * 4 + u) * 6 + 4 + idx, r1.at[h, u, idx], r1.at[h, u, 4 + idx], ring(d)
            )

    def send2(h, idx, src, d):
        c2[h, idx] = tr.send(48 + h * 6 + idx, src, r2.at[h, idx], halves[h][3](d))

    def close(u, h):
        pa, pb, _, _ = halves[h]
        tb = lax.rem(pb + OFFSETS[u], 4)
        for idx in (2, 3, 4, 5):
            c1[u, h, idx].wait_recv()
        p1[h, u, 0:2] = chunk(sums, h, pa, tb, 0)[...] + (r1[h, u, 3] + r1[h, u, 4])
        p1[h, u, 2:4] = chunk(sums, h, pa, tb, 1)[...] + (r1[h, u, 2] + r1[h, u, 5])
        if u == 0:
            send2(h, 0, p1.at[h, 0, pl.ds(0, 2)], 1)
            send2(h, 1, p1.at[h, 0, pl.ds(2, 2)], 3)
        if u == 1:
            send2(h, 3, p1.at[h, 1, pl.ds(0, 2)], 3)
            c2[h, 1].wait_recv()
            r2[h, 1] += p1[h, 1, 2:4]
            send2(h, 5, r2.at[h, 1], 3)
        if u == 2:
            send2(h, 2, p1.at[h, 2, pl.ds(2, 2)], 1)
            c2[h, 0].wait_recv()
            r2[h, 0] += p1[h, 2, 0:2]
            send2(h, 4, r2.at[h, 0], 1)

    both = range(2)
    for u in range(4):
        for h in both:
            send1(u, h, 0)
            send1(u, h, 1)
    def plain(u):
        for h in both:
            send1(u, h, 2)
            send1(u, h, 3)

    def on(u):
        for h in both:
            pass_on(u, h)

    def done(u):
        for h in both:
            close(u, h)

    plain(0)
    plain(1)
    hook(0)
    on(0)
    on(1)
    plain(2)
    plain(3)
    hook(1)
    on(2)
    done(0)
    on(3)
    done(1)
    done(2)
    done(3)
    hook(2)
    own = []
    for h in both:
        for idx in (2, 3, 4, 5):
            c2[h, idx].wait_recv()
        first = p1[h, 3, 0:2] + (r2[h, 3] + r2[h, 4])
        second = p1[h, 3, 2:4] + (r2[h, 2] + r2[h, 5])
        own += [first[0], first[1], second[0], second[1]]
    tr.finish()
    return jnp.concatenate(own, axis=1)


HOPS = ((0, None, 1), (0, None, 3), (3, 0, 1), (1, 1, 3))


def gather_all(vec, plane, tr, hook):
    halves = plane.halves
    order = (0, 3, 1, 2)
    c1, c2 = {}, {}

    def send1(h, idx):
        pa, pb, _, ring = halves[h]
        off, s, d = HOPS[idx]
        ref = chunk(vec, h, pa, lax.rem(pb + off, 4), s)
        c1[h, idx] = tr.send(RS_SLOTS + h * 4 + idx, ref, ref, ring(d))

    def send2(h, v, idx):
        pa, pb, ring, _ = halves[h]
        tb = lax.rem(pb + order[v], 4)
        off, s, d = HOPS[idx]
        ref = chunk(vec, h, lax.rem(pa + off, 4), tb, s)
        c2[h, v, idx] = tr.send(RS_SLOTS + 8 + (h * 4 + v) * 4 + idx, ref, ref, ring(d))

    both = range(2)

    def unit(v):
        for h in both:
            send2(h, v, 0)
            send2(h, v, 1)

    def pass_on(v):
        for h in both:
            for idx in range(2):
                c2[h, v, idx].wait_recv()
                send2(h, v, 2 + idx)

    for h in both:
        send1(h, 0)
        send1(h, 1)
    unit(0)
    hook(0)
    for h in both:
        for idx in range(2):
            c1[h, idx].wait_recv()
            send1(h, 2 + idx)
    unit(1)
    pass_on(0)
    unit(2)
    hook(1)
    for h in both:
        c1[h, 2].wait_recv()
        c1[h, 3].wait_recv()
    unit(3)
    pass_on(1)
    hook(2)
    pass_on(2)
    hook(3)
    pass_on(3)
    hook(4)
    for v in range(4):
        for h in both:
            c2[h, v, 2].wait_recv()
            c2[h, v, 3].wait_recv()
    tr.finish()


def sum_stages(row, col, n_row, n_col):
    plane = ([(lax.rem(row + d, n_row), col) for d in range(1, n_row)], row, n_row)
    across = ([(row, lax.rem(col + d, n_col)) for d in range(1, n_col)], col, n_col)
    return plane, across


class TileSum:
    def __init__(self, stages, tr, slot, box, rows):
        self.stages, self.tr, self.slot, self.box, self.rows = stages, tr, slot, box, rows
        self.at, self.open = 0, []

    def put(self, tile):
        peers, me, _ = self.stages[self.at]
        ref = self.box.at[self.at, me, pl.ds(0, self.rows)]
        self.box[self.at, me, 0 : self.rows] = tile
        self.open = []
        for device in peers:
            self.open.append(self.tr.send(self.slot, ref, ref, device))
            self.slot += 1

    def take(self):
        for c in self.open:
            c.wait_recv()
        total = self.box[self.at, 0, 0 : self.rows]
        for i in range(1, self.stages[self.at][2]):
            total = total + self.box[self.at, i, 0 : self.rows]
        self.at += 1
        return total

    def step(self):
        self.put(self.take())


GG, IG, MIX, STEP = range(4)
ROWS = 64
UNROLL = 8
LEAD = UNROLL * B
LOAD = 4
SLOTS = 4


def rows_loop(lo, hi, width, step):
    def some(o, carry):
        for j in range(width):
            step(lo + o * width + j)
        return carry

    lax.fori_loop(0, (hi - lo) // width, some, 0)


def cgls_kernel(n_row, n_col, table, blocks, targets, sol, res, *scratch):
    across, down, pieces, running, sums, vec, parts, images, t_mem, grads = scratch[:10]
    conj, gram_acc, small, r1, p1, r2, box, send_sem, recv_sem, load_sem, out_sem = scratch[10:]
    row, col = lax.axis_index("row"), lax.axis_index("col")
    plane = Plane(row, col)
    in_plane, across_it = sum_stages(row, col, n_row, n_col)
    tr, tr_small = Traffic(send_sem, recv_sem), Traffic(send_sem, recv_sem)

    size = LOAD * 16

    def load(step):
        slot = lax.rem(step, SLOTS)
        return pltpu.make_async_copy(
            blocks.at[pl.ds(step * size, size)], running.at[pl.ds(slot * size, size)], load_sem.at[slot]
        )

    read_targets = pltpu.make_async_copy(targets, t_mem, load_sem.at[SLOTS])
    read_targets.start()
    for s in range(SLOTS):
        load(s).start()

    barrier = pltpu.get_barrier_semaphore()
    who = in_plane[0] + across_it[0]
    for device in who:
        pl.semaphore_signal(barrier, inc=1, device_id=device, device_id_type=MESH)

    def lanes(i):
        return pl.ds(pl.multiple_of(i * B, B), B)

    def spot(i):
        return pl.ds(pl.multiple_of(LEAD + i * B, B), B)

    images[:, 0:LEAD] = jnp.zeros((2 * N * ITERS, LEAD), BF16)

    def piece(i, both, block):
        out = dot(jnp.concatenate([both, both], axis=1), block, 1, 0)
        out = out[:N] + out[N:]
        for k in range(4):
            pieces[i * 4 + k] = out[:, k * B : (k + 1) * B]

    read_targets.wait()

    def first(step, carry):
        load(step).wait()
        slot = lax.rem(step, SLOTS)
        for j in range(LOAD):
            i = step * LOAD + j
            his, los = [], []
            for k in range(4):
                base = slot * size + j * 16 + k * 4
                hi, lo = split(jnp.concatenate([running[base + q] for q in range(4)], axis=0))
                his.append(hi)
                los.append(lo)
            block = jnp.concatenate([jnp.concatenate(his, axis=1), jnp.concatenate(los, axis=1)], axis=0)
            across[i] = block
            piece(i, stacked(t_mem[:, lanes(i)]), block)

        @pl.when(step + SLOTS < ROWS // LOAD)
        def _():
            load(step + SLOTS).start()

        return carry

    lax.fori_loop(0, ROWS // LOAD, first, 0)

    def add_up():
        def run(o, total):
            for j in range(8):
                p = o * 8 + j
                total = jnp.where(table[FIRST, p] == 1, 0.0, total) + pieces[table[ORDER, p]]
                running[p] = total
            return total

        lax.fori_loop(0, ROWS * 4 // 8, run, jnp.zeros((N, B), F32))

        def pick(owner, carry):
            for h in range(2):
                for j in range(4):
                    c = owner * CBD + 4 * h + j
                    value = jnp.where(table[SOME, c] == 1, running[table[LAST, c]], 0.0)
                    sums[owner // 4, lax.rem(owner, 4), h, j] = value
            return carry

        lax.fori_loop(0, 16, pick, 0)

    def turn(i):
        for k in range(4):
            for h in range(2):
                tile = across[i, h * B : (h + 1) * B, k * B : (k + 1) * B]
                down[i, k * B : (k + 1) * B, h * B : (h + 1) * B] = tile.T

    def forward(at):
        def one(i):
            picked = jnp.concatenate([parts[table[COL, i * 4 + j]] for j in range(4)], axis=1)
            quad = dot(picked, down[i], 1, 0)
            quad = quad[:N] + quad[N:]
            images[at : at + 2 * N, spot(i)] = stacked(quad[:, :B] + quad[:, B:])

        return one

    def backward(at):
        def one(i):
            piece(i, images[at : at + 2 * N, spot(i)], across[i])

        return one

    def add_gram(k, group):
        at = pl.ds(pl.multiple_of(group * LEAD, LEAD), LEAD)
        mine = images[2 * N * k : 2 * N * (k + 1), at]
        gram_acc[:, 0 : 2 * N * (k + 1)] += dot(mine, images[0 : 2 * N * (k + 1), at], 1, 1)

    def forward_groups(k, lo, hi):
        row_of = forward(2 * N * k)

        def group(g, carry):
            add_gram(k, g)
            for j in range(UNROLL):
                row_of(g * UNROLL + j)
            return carry

        lax.fori_loop(lo, hi, group, 0)

    def image_grams(k):
        add_gram(k, ROWS // UNROLL)
        return jnp.concatenate(
            [pack(fold(gram_acc[:, 2 * N * j : 2 * N * (j + 1)])) for j in range(k, -1, -1)], axis=0
        )

    def mix_of(k):
        if k:
            small[k, MIX] = spd_solve(small[k - 1, GG], small[k, GG])

    def image_gram_of(k, total):
        gram = unpack(total[0:8])
        if k:
            mix = small[k, MIX]
            cross = unpack(total[8:16])
            if k == 2:
                cross = cross + exact(unpack(total[16:24]), small[1, MIX])
            mixed = exact(cross, mix)
            gram = gram + (mixed + mixed.T) + exact(mix, exact(small[k - 1, IG], mix), 0, 0)
        small[k, IG] = gram

    def cut(h, ta, tb):
        zz, xx = (tb, ta) if h == 0 else (ta, tb)
        for j in range(4):
            parts[(zz * 4 + xx) * CBD + 4 * h + j] = stacked(vec[zz, xx, h, j])

    def cut_unit(v, offsets):
        for h in range(2):
            pa, pb, _, _ = plane.halves[h]
            for off in offsets:
                cut(h, lax.rem(pa + off, 4), lax.rem(pb + (0, 3, 1, 2)[v], 4))

    add_up()
    pl.semaphore_wait(barrier, len(who))
    slot0 = RS_SLOTS + AG_SLOTS
    width = 1024
    strips = ROWS * B // width
    turned = {0: (0, 10), 1: (10, 22), 2: (22, 32)}
    turned_later = {0: (32, 36), 1: (36, 46), 2: (46, 52), 3: (52, 56), 4: (56, 64)}
    image_sum = None
    for k in range(ITERS):

        ready = []

        def beside_first(u, k=k, ready=ready):
            if k == 0:
                rows_loop(*turned[u], 2, turn)
            elif u == 0:
                mix_of(k - 1)
            elif u == 1:
                image_gram_of(k - 1, image_sum.take())
            else:
                step = spd_solve(small[k - 1, IG], small[k - 1, GG])
                small[k - 1, STEP] = step
                left = left_of([step])
                ready.append(left)
                if k == 1:
                    ready.append(grads[0])
                else:
                    known = halves_sum(left_of([small[1, MIX]]), stacked(conj[...]))
                    ready.append(grads[1] - halves_sum(left, stacked(known)))

        fresh = reduce_scatter(sums, plane, r1, p1, r2, tr, beside_first)
        if k == 0:
            grad = fresh
        else:
            grad = ready[1] - halves_sum(ready[0], stacked(fresh))
        for h in range(2):
            for j in range(4):
                at = (4 * h + j) * B
                vec[plane.z, plane.x, h, j] = grad[:, at : at + B]
        grad_sum = TileSum([across_it, in_plane], tr_small, slot0 + 2 * k * SUM_SLOTS, box.at[2 * k], 8)

        def beside_second(v, k=k):
            if v == 0:
                both = stacked(grad)
                grad_sum.put(pack(fold(dot(both, both, 1, 1))))
                grads[k] = grad
                if k == 1:
                    conj[...] = fresh
            else:
                cut_unit(v - 1, (0, 1, 3))
            if k == 0:
                rows_loop(*turned_later[v], 2, turn)

        gather_all(vec, plane, tr, beside_second)
        grad_sum.step()
        for v in range(4):
            cut_unit(v, (2,))
        gram_acc[...] = jnp.zeros_like(gram_acc)
        forward_groups(k, 0, ROWS // UNROLL)
        last = k + 1 == ITERS
        image_sum = TileSum(
            [in_plane, across_it],
            tr_small,
            slot0 + (2 * k + 1) * SUM_SLOTS,
            box.at[2 * k + 1],
            8 * (k + 1),
        )
        image_sum.put(image_grams(k))
        if not last:
            small[k, GG] = unpack(grad_sum.take())
            rows_loop(0, ROWS, UNROLL, backward(2 * N * k))
            add_up()
            image_sum.step()
        else:
            small[k, GG] = unpack(grad_sum.take())
            mix_of(k)
            mix = small[2, MIX]
            now = small[1, STEP]
            ahead = [exact(small[1, MIX], mix), mix]
            upto = [small[0, STEP] + exact(small[1, MIX], now), now]
            left = jnp.concatenate([left_of(ahead), left_of(upto)], axis=0)
            out = dot(left, jnp.concatenate([stacked(grads[j]) for j in range(2)], axis=0), 1, 0)
            grads[2] = grads[2] + (out[:N] + out[N : 2 * N])
            conj[...] = out[2 * N : 3 * N] + out[3 * N :]

            def prepare(s, carry, left=left):
                at = pl.ds(pl.multiple_of(s * width, width), width)
                there = pl.ds(pl.multiple_of(LEAD + s * width, width), width)
                out = dot(left, images[0 : 4 * N, there], 1, 0)
                own = images[4 * N : 5 * N, there].astype(F32) + images[5 * N : 6 * N, there].astype(F32)
                images[4 * N : 6 * N, there] = stacked(own + (out[:N] + out[N : 2 * N]))
                t_mem[:, at] = t_mem[:, at] - (out[2 * N : 3 * N] + out[3 * N :])
                return carry

            lax.fori_loop(0, ROWS * B // width, prepare, 0)
            image_sum.step()
            image_gram_of(k, image_sum.take())

    left = left_of([spd_solve(small[2, IG], small[2, GG])])
    conj[...] = conj[...] + halves_sum(left, stacked(grads[2]))
    out_sol = pltpu.make_async_copy(conj, sol, out_sem.at[strips])
    out_sol.start()

    def write(s):
        at = pl.ds(pl.multiple_of(s * width, width), width)
        return pltpu.make_async_copy(t_mem.at[:, at], res.at[:, at], out_sem.at[s])

    def finish(s, carry):
        at = pl.ds(pl.multiple_of(s * width, width), width)
        there = pl.ds(pl.multiple_of(LEAD + s * width, width), width)
        t_mem[:, at] = t_mem[:, at] - halves_sum(left, images[4 * N : 6 * N, there])
        write(s).start()
        return carry

    lax.fori_loop(0, strips, finish, 0)
    out_sol.wait()

    def wait(s, carry):
        write(s).wait()
        return carry

    lax.fori_loop(0, strips, wait, 0)
    tr_small.finish()


def body(blocks, block_cols, targets):
    n_row = lax.axis_size("row")
    n_col = lax.axis_size("col")
    group = CBD * n_row
    table = order_of(block_cols.reshape(1, -1), n_col)
    anywhere = pl.BlockSpec(memory_space=pl.ANY)
    width = CBD * B
    chunks = (4, 4, 2, CBD // 2, N, B)
    slots = RS_SLOTS + AG_SLOTS + 6 * SUM_SLOTS
    return tuple(
        pl.pallas_call(
            functools.partial(cgls_kernel, n_row, n_col),
            out_shape=[jax.ShapeDtypeStruct((N, width), F32), jax.ShapeDtypeStruct(targets.shape, F32)],
            in_specs=[pl.BlockSpec(memory_space=pltpu.SMEM), anywhere, anywhere],
            out_specs=[anywhere] * 2,
            scratch_shapes=[
                pltpu.VMEM((ROWS, 2 * B, 4 * B), BF16),
                pltpu.VMEM((ROWS, 4 * B, 2 * B), BF16),
                pltpu.VMEM((ROWS * 4, N, B), F32),
                pltpu.VMEM((ROWS * 4, N, B), F32),
                pltpu.VMEM(chunks, F32),
                pltpu.VMEM(chunks, F32),
                pltpu.VMEM((group, 2 * N, B), BF16),
                pltpu.VMEM((2 * N * ITERS, LEAD + ROWS * B), BF16),
                pltpu.VMEM((N, ROWS * B), F32),
                pltpu.VMEM((ITERS, N, width), F32),
                pltpu.VMEM((N, width), F32),
                pltpu.VMEM((2 * N, 2 * N * 4), F32),
                pltpu.VMEM((ITERS, 4, N, N), F32),
                pltpu.VMEM((2, 4, 6, 2, N, B), F32),
                pltpu.VMEM((2, 4, 4, N, B), F32),
                pltpu.VMEM((2, 6, 2, N, B), F32),
                pltpu.VMEM((6, 2, n_row, 24, B), F32),
                pltpu.SemaphoreType.DMA((slots,)),
                pltpu.SemaphoreType.DMA((slots,)),
                pltpu.SemaphoreType.DMA((SLOTS + 1,)),
                pltpu.SemaphoreType.DMA((ROWS * B // 1024 + 1,)),
            ],
            compiler_params=pltpu.CompilerParams(
                collective_id=0, has_side_effects=True, vmem_limit_bytes=60 * MIB
            ),
        )(table, blocks.reshape(-1, N, B), targets)
    )


def solution(mesh):
    placed = (P(("row", "col"), None, None, None), P(("row", "col"), None), P(None, ("row", "col")))
    return jax.shard_map(
        body,
        mesh=mesh,
        in_specs=placed,
        out_specs=(P(None, ("row", "col")), P(None, ("row", "col"))),
        check_vma=False,
    )
```
